32 devices in a mesh: dp: 4 (over x, core), seq: 8 (over z, y).
Axes of the slice: x: 2, y: 2, z: 4, core: 2. Of those that a mesh axis runs over, the one named last changes fastest.
Arguments:
- byte_embed: bfloat16 [16384, 1024], P(('dp', 'seq')), parts along dimension 0, may hold values from -6 to 6
- conv_taps: float32 [4, 1024], replicated, may hold values from -3 to 3
- norm_gain: float32 [4096], replicated, may hold values from 0.25 to 1.75
- w_qdown: bfloat16 [4096, 128], replicated
- w_qup: bfloat16 [128, 4096], replicated
- w_key: bfloat16 [4096, 256], replicated
- w_value: bfloat16 [4096, 256], replicated, may hold values from -0.09375 to 0.09375
- doc_lengths: int32 [64], P('dp'), parts along dimension 0, may hold values from 1 to 256, 1024 in all
- panel_dest: int32 [1024], P(('dp', 'seq')), parts along dimension 0, may hold values from 0 to 7, as said below
Outputs:
- rebalanced: bfloat16 [4096, 4096], P(('dp', 'seq')), parts along dimension 0
The draws below stay inside these ranges and needn't reach their ends.
There are 4 independent parts, one for each index of `dp`. The reference program is written for one: setup_inputs(seed, part) draws one part's arguments, and reference() takes and returns one part's arrays. A program takes and returns all parts, laid end to end along the dimension named above; an argument that names none is the same for every part. Nothing has to cross between parts.
Inputs may be any that keep to these rules, and one draw needn't show every extreme that they name: `doc_lengths`: the documents sum to 1024 shortened tokens and the longest has exactly 256. `panel_dest`: every index of seq receives exactly 32 panels; no index of seq sends more than 8 panels to one index of seq, and some pair reaches 8.
All inputs are finite; a program needn't handle non-finite values.
Results may differ from the reference program's by a relative error of at most 0.015.
Values may be sent and summed in bfloat16 or wider, within the bound.
No kernel may reach another device: no remote copies, remote signals or barrier semaphores. Data moves between devices by JAX's collectives and lax.ppermute only.
A program may use at most 64 MiB of HBM per device.

```python
import math
import jax
import jax.numpy as jnp
import numpy as np
from jax import lax

DB = 1024
H = 32
KVH = 2
SHORTEN = 4
KCONV = 4
PANEL = 4
TOK_DEV = 128
D = 4096
HD = 128
QRANK = 128
TOKENS = 1024
BYTES = 4096
PAN_DEV = 32
PANELS = 256
MOST = 8
MAXDOC = 256
DOCS = 16
N_SEQ = 8


def draw_w_key(key, part):
    noise_part = jax.random.normal(jax.random.fold_in(key, 14), (D, KVH * HD), jnp.float32) * D ** (-0.5)
    weights = noise_part
    return weights.astype(jnp.bfloat16)


def draw_w_qdown(key, part):
    noise_part = jax.random.normal(jax.random.fold_in(key, 12), (D, QRANK), jnp.float32) * D ** (-0.5)
    weights = noise_part
    return weights.astype(jnp.bfloat16)


def draw_w_qup(key, part):
    noise_part = jax.random.normal(jax.random.fold_in(key, 15), (QRANK, D), jnp.float32) * QRANK ** (-0.5)
    weights = noise_part
    return weights.astype(jnp.bfloat16)


def draw_panel_dest(key, part):
    k_src, k_dst, k_shift, k_order = jax.random.split(key, 4)
    source_place = jax.random.permutation(k_src, N_SEQ)
    dest_owner = jax.random.permutation(k_dst, N_SEQ)
    shift_vals = jax.random.permutation(k_shift, N_SEQ)
    shifts = shift_vals[jnp.arange(PAN_DEV) // MOST]

    def one_order(sub_key):
        return jax.random.permutation(sub_key, PAN_DEV)
    orders = jax.vmap(one_order)(jax.random.split(k_order, N_SEQ))
    destination = dest_owner[(source_place[:, None] + shifts[orders]) % N_SEQ]
    return destination.reshape(-1).astype(jnp.int32)


def block_levels(own_key, dims, pieces, least, top_value):
    level = 1.0
    for axis_at, parts in pieces:
        steps = jax.random.uniform(jax.random.fold_in(jax.random.fold_in(own_key, 6), axis_at), (parts,), jnp.float32, least / len(pieces), top_value / len(pieces))
        level = level * jnp.repeat(jnp.exp(steps), dims[axis_at] // parts).reshape((-1,) + (1,) * (len(dims) - 1 - axis_at))
    return level


def profile(count, total, limit, lean):
    portions = [(1 << 20) // math.isqrt(standing ** lean) + 1 for standing in range(2, count + 1)]
    rest, holding = total - limit - (count - 1), [1] * (count - 1)
    while rest > 0:
        candidates = [i for i in range(count - 1) if holding[i] < limit]
        mass, left = sum([portions[i] for i in candidates]), rest
        for i in candidates:
            extra = min(limit - holding[i], max(1, left * portions[i] // mass), rest)
            holding[i] = holding[i] + extra
            rest = rest - extra
    return np.array([limit] + holding)


def uneven_parts(stream_key, number_of, total, bound, slope):
    if number_of == 2:
        one = jax.random.randint(stream_key, (), max(1, total - bound), min(bound, total - 1) + 1)
        return jnp.stack([one, total - one])
    tallies = jnp.asarray(profile(number_of, total, bound, slope), jnp.int32)
    twos = (number_of - 1) // 2
    giver, sink = tallies[1:1 + 2 * twos:2], tallies[2:2 + 2 * twos:2]
    room = jnp.minimum(giver - 1, bound - sink)
    passed = jax.random.randint(jax.random.fold_in(stream_key, 1), (twos,), 0, 1 << 20) % (room + 1)
    tallies = tallies.at[1:1 + 2 * twos:2].set(giver - passed).at[2:2 + 2 * twos:2].set(sink + passed)
    return tallies[jax.random.permutation(jax.random.fold_in(stream_key, 2), number_of)]


def normal_values(own_key, extent, width, limit, pieces=(), held_as=jnp.bfloat16):
    values = jax.random.normal(own_key, extent, jnp.float32) * width
    if len(pieces) > 0:
        values = block_levels(own_key, extent, pieces, -0.22, 0.18) * values
    return jnp.clip(values, min=-limit, max=limit).astype(held_as)


def setup_inputs(seed: int = 0, part: int = 0) -> dict:
    key_list = jax.random.split(jax.random.key(seed), 10)
    part_keys = jax.random.split(jax.random.fold_in(key_list[9], part), 10)
    byte_embed = normal_values(part_keys[0], (BYTES, DB), 1.0, 6.0, ((0, 8),))
    conv_taps = normal_values(key_list[1], (KCONV, DB), 0.5, 3.0, (), jnp.float32)
    norm_gain = jnp.clip(1.0 + 0.15 * jax.random.normal(key_list[2], (D,), jnp.float32), 0.25, 1.75)
    w_qdown = draw_w_qdown(jax.random.fold_in(key_list[9], 71), part)
    w_qup = draw_w_qup(jax.random.fold_in(key_list[9], 71), part)
    w_key = draw_w_key(jax.random.fold_in(key_list[9], 71), part)
    w_value = normal_values(key_list[6], (D, KVH * HD), D ** -0.5, 0.09375)
    doc_lengths = uneven_parts(part_keys[7], DOCS, TOKENS, MAXDOC, 2).astype(jnp.int32)
    panel_dest = draw_panel_dest(jax.random.fold_in(jax.random.fold_in(key_list[9], part), 71), part)
    return dict(byte_embed=byte_embed, conv_taps=conv_taps, norm_gain=norm_gain, w_qdown=w_qdown, w_qup=w_qup, w_key=w_key, w_value=w_value, doc_lengths=doc_lengths, panel_dest=panel_dest)


def doc_index(positions, doc_ends):
    return lax.optimization_barrier(jnp.sum((positions[:, None] >= doc_ends[None, :]).astype(jnp.int32), axis=1))

def reference(byte_embed, conv_taps, norm_gain, w_qdown, w_qup, w_key, w_value, doc_lengths, panel_dest):
    doc_ends = jnp.cumsum(doc_lengths).astype(jnp.int32)
    token_doc = doc_index(jnp.arange(TOKENS, dtype=jnp.int32), doc_ends)
    byte_doc = jnp.repeat(token_doc, SHORTEN, total_repeat_length=BYTES)
    padded = jnp.concatenate([jnp.zeros((KCONV - 1, DB), byte_embed.dtype), byte_embed], axis=0)
    padded_doc = jnp.concatenate([jnp.full((KCONV - 1,), -1, jnp.int32), byte_doc])
    conv_sum = jnp.zeros((BYTES, DB), jnp.float32)
    for tap_index in range(KCONV):
        begin_at = KCONV - 1 - tap_index
        window = padded[begin_at:begin_at + BYTES].astype(jnp.float32)
        same_doc = padded_doc[begin_at:begin_at + BYTES] == byte_doc
        conv_sum = conv_sum + jnp.where(same_doc[:, None], window * conv_taps[tap_index][None, :].astype(jnp.float32), 0.0)
    shortened = conv_sum.reshape(TOKENS, D).astype(jnp.bfloat16)
    short_wide = shortened.astype(jnp.float32)
    mean_sq = lax.optimization_barrier(jnp.mean(short_wide * short_wide, axis=1, keepdims=True))
    normed = (short_wide * lax.rsqrt(mean_sq + 1e-06) * norm_gain[None, :].astype(jnp.float32)).astype(jnp.bfloat16)
    latent = jnp.dot(normed, w_qdown, preferred_element_type=jnp.float32).astype(jnp.bfloat16)
    query = jnp.dot(latent, w_qup, preferred_element_type=jnp.float32).astype(jnp.bfloat16)
    groups = H // KVH
    query = query.reshape(TOKENS, KVH, groups, HD)
    key_all = jnp.dot(normed, w_key, preferred_element_type=jnp.float32).astype(jnp.bfloat16).reshape(TOKENS, KVH, HD)
    value_all = jnp.dot(normed, w_value, preferred_element_type=jnp.float32).astype(jnp.bfloat16).reshape(TOKENS, KVH, HD)
    key_pad = jnp.concatenate([jnp.zeros((2 * TOK_DEV, KVH, HD), jnp.bfloat16), key_all], axis=0)
    value_pad = jnp.concatenate([jnp.zeros((2 * TOK_DEV, KVH, HD), jnp.bfloat16), value_all], axis=0)
    score_scale = 1.0 / math.sqrt(HD)

    def block(block_index):
        first = (block_index * TOK_DEV).astype(jnp.int32)
        query_blk = lax.dynamic_slice_in_dim(query, first, TOK_DEV, 0).astype(jnp.float32)
        key_blk = lax.dynamic_slice_in_dim(key_pad, first, 3 * TOK_DEV, 0).astype(jnp.float32)
        value_blk = lax.dynamic_slice_in_dim(value_pad, first, 3 * TOK_DEV, 0).astype(jnp.float32)
        query_pos = first + jnp.arange(TOK_DEV, dtype=jnp.int32)
        key_pos = first - 2 * TOK_DEV + jnp.arange(3 * TOK_DEV, dtype=jnp.int32)
        query_doc = doc_index(query_pos, doc_ends)
        key_doc = doc_index(key_pos, doc_ends)
        allowed = (key_pos[None, :] <= query_pos[:, None]) & (key_pos[None, :] >= 0) & (key_doc[None, :] == query_doc[:, None])
        scores = jnp.einsum('qkge,jke->kgqj', query_blk, key_blk) * score_scale
        scores = jnp.where(allowed[None, None], scores, -1e+30)
        row_max = lax.optimization_barrier(jnp.max(scores, axis=3, keepdims=True))
        exp_scores = jnp.exp(scores - row_max)
        attn_probs = (exp_scores / lax.optimization_barrier(jnp.sum(exp_scores, axis=3, keepdims=True))).astype(jnp.bfloat16)
        mixed = jnp.einsum('kgqj,jke->qkge', attn_probs.astype(jnp.float32), value_blk)
        return mixed.reshape(TOK_DEV, D)
    attended = lax.map(block, jnp.arange(N_SEQ, dtype=jnp.int32)).reshape(TOKENS, D)
    layer_out = (short_wide + attended).astype(jnp.bfloat16)
    panel_order = jnp.argsort(panel_dest, stable=True)
    placed = layer_out.reshape(PANELS, PANEL, D)[panel_order]
    return placed.reshape(TOKENS, D)
```

```python
import functools
import math

import jax
import jax.numpy as jnp
from jax import lax
from jax.experimental import pallas as pl
from jax.experimental.pallas import tpu as pltpu
from jax.sharding import PartitionSpec as P

H = 32
SHORTEN = 4
KCONV = 4
PANEL = 4
PAD = 8
EDGE = 16
VMEM_BYTES = 48 * 1024 * 1024
F32 = jnp.float32
BF16 = jnp.bfloat16


def iota(shape, dim):
    return lax.broadcasted_iota(jnp.int32, shape, dim)


def reverse_bits(value, bits):
    out = value * 0
    for b in range(bits):
        out = out + (((value >> b) & 1) << (bits - 1 - b))
    return out


def conv_kernel(n_seq, rows, merged, me_ref, lens_ref, dest_ref, x_ref, taps_ref, *refs):
    n_out = 1 if merged else n_seq
    block_refs = refs[:n_out]
    short_ref, corr_ref, wide_ref, keep_ref, pick_ref = refs[n_out:]
    n_bytes, byte_dim = x_ref.shape
    toks = n_bytes // SHORTEN
    slot = pl.program_id(0)
    me = me_ref[0]

    @pl.when(slot == 0)
    def _():
        for c in range(byte_dim // 128):
            wide_ref[c, 0:PAD, :] = jnp.zeros((PAD, 128), F32)
            wide_ref[c, PAD + n_bytes :, :] = jnp.zeros((PAD, 128), F32)
            wide_ref[c, PAD : PAD + n_bytes, :] = x_ref[:, c * 128 : (c + 1) * 128].astype(F32)
        token = me * toks + iota((toks + 8, 128), 0)

        def doc(d, carry):
            first, keep = carry
            return first + lens_ref[d], jnp.where(token == first, 0.0, keep)

        _, keep = lax.fori_loop(
            0, lens_ref.shape[0], doc, (jnp.int32(0), jnp.ones((toks + 8, 128), F32))
        )
        keep_ref[...] = keep
        lane = iota((8, toks), 1)
        panel = lane // PANEL
        dest = jnp.full((8, toks), -1, jnp.int32)
        for p in range(toks // PANEL):
            dest = jnp.where(panel == p, dest_ref[p], dest)
        rank = jnp.zeros((8, toks), jnp.int32)
        for p in range(toks // PANEL):
            rank = rank + jnp.where((panel > p) & (dest == dest_ref[p]), 1, 0)
        place = (dest ^ me) * rows + rank * PANEL + lane % PANEL
        row = iota((n_seq * rows, toks), 0)
        pick_ref[...] = jnp.where(row == place[0:1], 1.0, 0.0).astype(BF16)

    for c in range(byte_dim // 128):
        cols = slice(c * 128, (c + 1) * 128)
        total = jnp.zeros((toks, 128), F32)
        corr = jnp.zeros((1, 128), F32)
        for tap in range(KCONV):
            weight = taps_ref[tap : tap + 1, cols]
            part = wide_ref[c, pl.ds(PAD + slot - tap, toks, stride=SHORTEN), :] * weight
            if tap > 0:
                part = part * jnp.where(slot < tap, keep_ref[0:toks, :], 1.0)
                corr = corr + wide_ref[c, pl.ds(PAD + n_bytes + slot - tap, 1), :] * weight
            total = total + part
        corr_ref[:, cols] = jnp.broadcast_to(corr * keep_ref[toks : toks + 1, :], (8, 128))
        short_ref[:, cols] = total.astype(BF16)
    step = min(256, byte_dim)
    for at in range(0, byte_dim, step):
        cols = slice(at, at + step)
        placed = jnp.dot(pick_ref[...], short_ref[:, cols], preferred_element_type=F32).astype(BF16)
        if merged:
            block_refs[0][:, cols] = placed
        else:
            for k in range(n_seq):
                block_refs[k][:, cols] = placed[k * rows : (k + 1) * rows]


def project_kernel(
    dest_ref, short_ref, corr_ref, gain_ref, wk_ref, wv_ref, wd_ref, out_ref, rs_ref, acc_ref, edge_ref
):
    toks, width = short_ref.shape
    depth = wk_ref.shape[0]
    at = pl.program_id(0)
    kv = wk_ref.shape[1]

    @pl.when(at == 0)
    def _():
        total = jnp.zeros((toks, 128), F32)
        for c in range(0, width, 128):
            piece = short_ref[:, c : c + 128].astype(F32)
            total = total + piece * piece
        mean = jnp.sum(total, axis=1, keepdims=True) * (1.0 / width)
        rs_ref[...] = jnp.broadcast_to(lax.rsqrt(mean + 1e-06), (toks, 128))
        acc_ref[...] = jnp.zeros_like(acc_ref)

    cols = pl.ds(pl.multiple_of(at * depth, depth), depth)
    piece = short_ref[:, cols].astype(F32)
    gain = gain_ref[:, cols]
    normed = (piece * rs_ref[:, 0:1] * gain).astype(BF16)
    row = iota((EDGE, depth), 0)
    edge = jnp.where(row == 0, piece[0:1], jnp.where(row == 1, corr_ref[0:1, cols], 0.0)) * gain
    left = jnp.concatenate([normed, edge.astype(BF16)], axis=0)
    acc_ref[:, 0:kv] += jnp.dot(left, wk_ref[...], preferred_element_type=F32)
    acc_ref[:, kv : 2 * kv] += jnp.dot(left, wv_ref[...], preferred_element_type=F32)
    acc_ref[:, 2 * kv :] += jnp.dot(left, wd_ref[...], preferred_element_type=F32)

    @pl.when(at == pl.num_programs(0) - 1)
    def _():
        out_ref[0 : toks + EDGE, :] = acc_ref[...].astype(BF16)
        row = iota((EDGE, 128), 0)
        lane = iota((EDGE, 128), 1)
        dest = jnp.zeros((EDGE, 128), F32)
        for p in range(dest_ref.shape[0]):
            dest = jnp.where(lane == p, dest_ref[p].astype(F32), dest)
        low = acc_ref[toks : toks + EDGE, 0:128]
        out_ref[toks : toks + EDGE, 0:128] = jnp.where(row == 2, dest, low).astype(BF16)
        part = width // 8
        for c in range(8):
            edge_ref[c : c + 1, :] = short_ref[0:EDGE, c * part : (c + 1) * part].astype(F32)[0:1]
            edge_ref[8 + c : 9 + c, :] = corr_ref[0:1, c * part : (c + 1) * part]
        out_ref[toks + EDGE : toks + 2 * EDGE, 0:part] = edge_ref[...].astype(BF16)


def attend_kernel(
    n_seq, rows, pans, stack, me_ref, lens_ref, all_ref, wq_ref, add_ref, sel_ref,
    k_ref, v_ref, lat_ref, bias_ref, pick_ref, corr_ref, mine_ref,
):
    bits = n_seq.bit_length() - 1
    toks = lat_ref.shape[0]
    hd = lat_ref.shape[1]
    kvh = k_ref.shape[0]
    kv = kvh * hd
    width = corr_ref.shape[1]
    part = width // 8
    heads = wq_ref.shape[1] // hd
    keys = n_seq * toks
    me = me_ref[0]
    step = pl.program_id(0)

    @pl.when(step == 0)
    def _():
        perm = [int(reverse_bits(q, bits)) for q in range(n_seq)]
        shards = [me ^ perm[q] for q in range(n_seq)]
        mine_ref[...] = jnp.zeros_like(mine_ref)
        corr_ref[...] = jnp.zeros_like(corr_ref)
        lane128 = iota((1, 128), 1)
        me_f = me.astype(F32)
        latents = []
        top_row = iota((EDGE, 2 * kv + hd), 0)
        for q in range(n_seq):
            shard = shards[q]
            live = shard > 0
            before = reverse_bits(me ^ jnp.where(live, shard - 1, shard), bits)
            live = jnp.where(live, 1.0, 0.0)
            corr = all_ref[before, toks + EDGE : toks + 2 * EDGE, 0:part].astype(F32)[8:16] * live
            own = all_ref[q, toks + EDGE : toks + 2 * EDGE, 0:part].astype(F32)[0:8]
            first = (own + corr).astype(BF16).astype(F32)
            mean = jnp.sum(jnp.sum(first * first, axis=1, keepdims=True), axis=0, keepdims=True) * (1.0 / width)
            info = all_ref[q, toks : toks + EDGE, :].astype(F32)
            past = all_ref[before, toks : toks + EDGE, :].astype(F32)
            fixed = lax.rsqrt(mean + 1e-06) * (info[0:1] + past[1:2] * live)
            top = jnp.where(top_row == 0, fixed, all_ref[q, 0:EDGE, :].astype(F32)).astype(BF16)
            for g in range(kvh):
                at = slice(g * hd, (g + 1) * hd)
                k_ref[g, q * toks : q * toks + EDGE, :] = top[:, at]
                k_ref[g, q * toks + EDGE : (q + 1) * toks, :] = all_ref[q, EDGE:toks, at]
                at = slice(kv + g * hd, kv + (g + 1) * hd)
                v_ref[g, q * toks : q * toks + EDGE, 0:hd] = top[:, at]
                v_ref[g, q * toks + EDGE : (q + 1) * toks, 0:hd] = all_ref[q, EDGE:toks, at]
                v_ref[g, q * toks : (q + 1) * toks, hd:] = jnp.ones((toks, hd), BF16)
            latents.append(jnp.concatenate([top[:, 2 * kv :], all_ref[q, EDGE:toks, 2 * kv :]], axis=0))
            for c in range(8):
                corr_ref[q : q + 1, c * part : (c + 1) * part] = corr[c : c + 1]
            mine_ref[q : q + 1, :] = jnp.where((info[2:3, 0:128] == me_f) & (lane128 < pans), 1.0, 0.0)
        mine = mine_ref[...]
        n_pad = mine.shape[0]
        count = jnp.sum(mine, axis=1, keepdims=True)
        shard_col = me ^ reverse_bits(iota((n_pad, 1), 0), bits)
        offset = jnp.zeros((n_pad, 1), F32)
        for q in range(n_seq):
            offset = offset + jnp.where(shard_col > shards[q], count[q : q + 1], 0.0)
        pan_row, tok_lane = iota((128, toks), 0), iota((128, toks), 1)
        below = jnp.where(pan_row < tok_lane // PANEL, 1.0, 0.0).astype(BF16)
        equal = jnp.where(pan_row == tok_lane // PANEL, 1.0, 0.0).astype(BF16)
        mine16 = mine.astype(BF16)
        rank = jnp.dot(mine16, below, preferred_element_type=F32)
        chosen = jnp.dot(mine16, equal, preferred_element_type=F32)
        lane = iota((n_pad, toks), 1)
        place = jnp.where(chosen > 0.5, PANEL * (offset + rank) + (lane % PANEL).astype(F32), -1.0)
        out_row = iota((toks, toks), 0).astype(F32)
        tok = iota((toks, toks), 1)
        latent = jnp.zeros((toks, hd), F32)
        where_at = jnp.zeros((toks, toks), F32)
        pick = jnp.zeros(pick_ref.shape, F32)
        pick_lane = iota(pick_ref.shape, 1)
        for q in range(n_seq):
            hit = jnp.where(out_row == place[q : q + 1], 1.0, 0.0)
            latent = latent + jnp.dot(hit.astype(BF16), latents[q], preferred_element_type=F32)
            where_at = where_at + hit * (shards[q] * toks + tok).astype(F32)
            pick = jnp.where(pick_lane == q, hit[:, 0:1], pick)
        lat_ref[...] = latent.astype(BF16)
        pick_ref[...] = pick.astype(BF16)
        pos = jnp.broadcast_to(jnp.sum(where_at, axis=1, keepdims=True), (toks, 128)).astype(jnp.int32)

        def doc(d, carry):
            first, begin = carry
            return first + lens_ref[d], jnp.where(pos >= first, first, begin)

        _, begin = lax.fori_loop(
            0, lens_ref.shape[0], doc, (jnp.int32(0), jnp.zeros((toks, 128), jnp.int32))
        )
        for q in range(n_seq):
            key = shards[q] * toks + tok
            bias_ref[:, q * toks : (q + 1) * toks] = jnp.where(
                (key >= begin[:, 0:1]) & (key <= pos[:, 0:1]), 0.0, -1e30
            )
        slot_lane = iota((1, n_seq * rows), 1)
        within = slot_lane % rows
        target = jnp.full((1, n_seq * rows), -1.0, F32)
        for q in range(n_seq):
            valid = (slot_lane // rows == perm[q]) & ((within // PANEL).astype(F32) < count[q : q + 1])
            target = jnp.where(valid, PANEL * offset[q : q + 1] + within.astype(F32), target)
        sel_row = iota((toks, n_seq * rows), 0).astype(F32)
        sel_ref[...] = jnp.where(sel_row == target, 1.0, 0.0).astype(BF16)

    scale = math.log2(math.e) / math.sqrt(hd)
    group = step // (pl.num_programs(0) // kvh)
    query = (jnp.dot(lat_ref[...], wq_ref[...], preferred_element_type=F32) * scale).astype(BF16)
    key_all, value_all = k_ref[group], v_ref[group]
    outs = []
    for h in range(0, heads, stack):
        rows_q = jnp.concatenate([query[:, (h + i) * hd : (h + i + 1) * hd] for i in range(stack)], axis=0)
        scores = lax.dot_general(rows_q, key_all, (((1,), (1,)), ((), ())), preferred_element_type=F32)
        scores = scores.reshape(stack, toks, keys) + bias_ref[...][None]
        top = jnp.max(scores, axis=2, keepdims=True)
        probs = jnp.exp2(scores - top).astype(BF16).reshape(stack * toks, keys)
        mixed = jnp.dot(probs, value_all, preferred_element_type=F32)
        mixed = mixed[:, 0:hd] / mixed[:, hd:]
        outs += [mixed[i * toks : (i + 1) * toks] for i in range(stack)]
    wide = heads * hd
    cols = pl.ds(pl.multiple_of(step * wide, wide), wide)
    extra = jnp.dot(pick_ref[...], corr_ref[:, cols].astype(BF16), preferred_element_type=F32)
    add_ref[...] = jnp.concatenate(outs, axis=1) + extra


def place_kernel(sel_ref, add_ref, *refs):
    out_ref = refs[-1]
    blocks = [r[...] for r in refs[:-1]]
    rows = blocks[0] if len(blocks) == 1 else jnp.concatenate(blocks, axis=0)
    out_ref[...] = (jnp.dot(sel_ref[...], rows, preferred_element_type=F32) + add_ref[...]).astype(BF16)


def swap(array, by, size):
    return lax.ppermute(array, "seq", [(i, i ^ by) for i in range(size)])


def smem():
    return pl.BlockSpec(memory_space=pltpu.SMEM)


def whole_block(shape):
    return pl.BlockSpec(shape, lambda i: (0,) * len(shape))


def column_block(rows, cols):
    return pl.BlockSpec((rows, cols), lambda i: (0, i))


def params():
    return pltpu.CompilerParams(vmem_limit_bytes=VMEM_BYTES, dimension_semantics=("arbitrary",))


def per_device(
    byte_embed, conv_taps, norm_gain, w_qdown, w_qup, w_key, w_value, doc_lengths, panel_dest
):
    n_seq = lax.axis_size("seq")
    bits = n_seq.bit_length() - 1
    me = lax.axis_index("seq").astype(jnp.int32).reshape(1)
    n_bytes, byte_dim = byte_embed.shape
    toks = n_bytes // SHORTEN
    width = SHORTEN * byte_dim
    hd = width // H
    kv = w_key.shape[1]
    kvh = kv // hd
    rank = w_qdown.shape[1]
    pans = toks // PANEL
    slots = (2 * pans + n_seq - 1) // n_seq
    rows = slots * PANEL
    merged = rows % 16 != 0
    wide = 2 * kv + rank

    block_rows = n_seq * rows if merged else rows
    n_out = 1 if merged else n_seq
    *blocks, short, corr = pl.pallas_call(
        functools.partial(conv_kernel, n_seq, rows, merged),
        grid=(SHORTEN,),
        out_shape=[jax.ShapeDtypeStruct((block_rows, width), BF16)] * n_out
        + [jax.ShapeDtypeStruct((toks, width), BF16), jax.ShapeDtypeStruct((8, width), F32)],
        in_specs=[smem(), smem(), smem(), whole_block(byte_embed.shape), whole_block(conv_taps.shape)],
        out_specs=[column_block(block_rows, byte_dim)] * n_out
        + [column_block(toks, byte_dim), column_block(8, byte_dim)],
        scratch_shapes=[
            pltpu.VMEM((byte_dim // 128, n_bytes + 2 * PAD, 128), F32),
            pltpu.VMEM((toks + 8, 128), F32),
            pltpu.VMEM((n_seq * rows, toks), BF16),
        ],
        compiler_params=params(),
        name="conv_panels",
    )(me, doc_lengths, panel_dest, byte_embed, conv_taps)
    if merged:
        blocks = [blocks[0][k * rows : (k + 1) * rows] for k in range(n_seq)]

    depth = width // 4
    held = pl.pallas_call(
        project_kernel,
        grid=(width // depth,),
        out_shape=jax.ShapeDtypeStruct((toks + 2 * EDGE, wide), BF16),
        in_specs=[
            smem(),
            whole_block((toks, width)),
            whole_block((8, width)),
            whole_block((1, width)),
            pl.BlockSpec((depth, kv), lambda i: (i, 0)),
            pl.BlockSpec((depth, kv), lambda i: (i, 0)),
            pl.BlockSpec((depth, rank), lambda i: (i, 0)),
        ],
        out_specs=whole_block((toks + 2 * EDGE, wide)),
        scratch_shapes=[
            pltpu.VMEM((toks, 128), F32),
            pltpu.VMEM((toks + EDGE, wide), F32),
            pltpu.VMEM((16, width // 8), F32),
        ],
        compiler_params=params(),
        name="project",
    )(panel_dest, short, corr, norm_gain.reshape(1, width), w_key, w_value, w_qdown)

    held = held[None]
    for b in range(bits - 1, -1, -1):
        held = jnp.concatenate([held, swap(held, 1 << b, n_seq)], axis=0)

    got = {0: blocks[0]}
    for k in list(range(n_seq // 2, n_seq)) + list(range(1, n_seq // 2)):
        got[k] = swap(blocks[k], k, n_seq)

    heads = min(4, H // kvh)
    stack = heads if n_seq * toks <= 1024 else 1
    n_pad = max(16, n_seq)
    added, sel = pl.pallas_call(
        functools.partial(attend_kernel, n_seq, rows, pans, stack),
        grid=(H // heads,),
        out_shape=[
            jax.ShapeDtypeStruct((toks, width), F32),
            jax.ShapeDtypeStruct((toks, n_seq * rows), BF16),
        ],
        in_specs=[smem(), smem(), whole_block(held.shape), column_block(rank, heads * hd)],
        out_specs=[column_block(toks, heads * hd), whole_block((toks, n_seq * rows))],
        scratch_shapes=[
            pltpu.VMEM((kvh, n_seq * toks, hd), BF16),
            pltpu.VMEM((kvh, n_seq * toks, 2 * hd), BF16),
            pltpu.VMEM((toks, rank), BF16),
            pltpu.VMEM((toks, n_seq * toks), F32),
            pltpu.VMEM((toks, n_pad), BF16),
            pltpu.VMEM((n_pad, width), F32),
            pltpu.VMEM((n_pad, 128), F32),
        ],
        compiler_params=params(),
        name="attend",
    )(me, doc_lengths, held, w_qup)

    arrived = [got[k] for k in range(n_seq)]
    if merged:
        arrived = [jnp.concatenate(arrived, axis=0)]
    out_cols = width // 4
    return pl.pallas_call(
        place_kernel,
        grid=(4,),
        out_shape=jax.ShapeDtypeStruct((toks, width), BF16),
        in_specs=[whole_block(sel.shape), column_block(toks, out_cols)]
        + [column_block(a.shape[0], out_cols) for a in arrived],
        out_specs=column_block(toks, out_cols),
        compiler_params=params(),
        name="place",
    )(sel, added, *arrived)


def solution(mesh):
    in_specs = (P(("dp", "seq"), None), P(), P(), P(), P(), P(), P(), P("dp"), P(("dp", "seq")))
    out_specs = P(("dp", "seq"), None)
    return jax.shard_map(
        per_device, mesh=mesh, in_specs=in_specs, out_specs=out_specs, check_vma=False
    )
```

```python
import functools
import math

import jax
import jax.numpy as jnp
from jax import lax
from jax.experimental import pallas as pl
from jax.experimental.pallas import tpu as pltpu
from jax.sharding import PartitionSpec as P

H = 32
SHORTEN = 4
KCONV = 4
PANEL = 4
BACK = 2
PAD = 8
EDGE = 16
MARK = 2.0**120
VMEM_BYTES = 48 * 1024 * 1024
ALL_VMEM = 60 * 1024 * 1024
F32 = jnp.float32
BF16 = jnp.bfloat16


def iota(shape, dim):
    return lax.broadcasted_iota(jnp.int32, shape, dim)


def project_kernel(
    me_ref, lens_hbm, x_hbm, taps_hbm, gain_hbm, wk_hbm, wv_hbm, wd_hbm,
    out_ref, short_ref, lat_ref, edge_ref,
    lens_ref, x_ref, taps_ref, gain_ref, w_ref, sems, wsems, wide_ref, keep_ref, u_ref, acc_ref, fold_ref,
):
    n_bytes, byte_dim = x_ref.shape
    toks, width = short_ref.shape
    kv = wk_hbm.shape[1]
    rank = wd_hbm.shape[1]
    me = me_ref[0]
    small = [
        pltpu.make_async_copy(lens_hbm, lens_ref, sems.at[0]),
        pltpu.make_async_copy(taps_hbm, taps_ref, sems.at[1]),
        pltpu.make_async_copy(gain_hbm, gain_ref, sems.at[2]),
    ]
    some = n_bytes // 4
    large = [
        pltpu.make_async_copy(
            x_hbm.at[pl.ds(i * some, some)], x_ref.at[pl.ds(i * some, some)], sems.at[3 + i]
        )
        for i in range(4)
    ]
    weights = []
    for i in range(SHORTEN):
        at = pl.ds(i * byte_dim, byte_dim)
        weights.append(
            [
                pltpu.make_async_copy(wk_hbm.at[at], w_ref.at[at, pl.ds(0, kv)], wsems.at[i, 0]),
                pltpu.make_async_copy(wv_hbm.at[at], w_ref.at[at, pl.ds(kv, kv)], wsems.at[i, 1]),
                pltpu.make_async_copy(wd_hbm.at[at], w_ref.at[at, pl.ds(2 * kv, rank)], wsems.at[i, 2]),
            ]
        )
    for copy in small + large + [copy for group in weights for copy in group]:
        copy.start()
    for c in range(byte_dim // 128):
        wide_ref[c, 0:PAD, :] = jnp.zeros((PAD, 128), F32)
        wide_ref[c, PAD + n_bytes :, :] = jnp.zeros((PAD, 128), F32)
    u_ref[toks:, :] = jnp.zeros((EDGE, width), BF16)
    for copy in small:
        copy.wait()
    token = me * toks + iota((toks + 8, 128), 0)

    def doc(d, carry):
        first, keep = carry
        return first + lens_ref[d], jnp.where(token == first, 0.0, keep)

    _, keep = lax.fori_loop(
        0, lens_ref.shape[0], doc, (jnp.int32(0), jnp.ones((toks + 8, 128), F32))
    )
    keep_ref[...] = keep
    for i, copy in enumerate(large):
        copy.wait()
        for c in range(byte_dim // 128):
            wide_ref[c, PAD + i * some : PAD + (i + 1) * some, :] = x_ref[
                i * some : (i + 1) * some, c * 128 : (c + 1) * 128
            ].astype(F32)

    part = width // 8
    squares = jnp.zeros((toks, 128), F32)
    for slot in range(SHORTEN):
        for c in range(byte_dim // 128):
            cols = slice(c * 128, (c + 1) * 128)
            at = slot * byte_dim + c * 128
            here = jnp.zeros((toks, 128), F32)
            before = jnp.zeros((toks, 128), F32)
            corr = jnp.zeros((1, 128), F32)
            for tap in range(KCONV):
                weight = taps_ref[tap : tap + 1, cols]
                term = wide_ref[c, pl.ds(PAD + slot - tap, toks, stride=SHORTEN), :] * weight
                if tap > slot:
                    before = before + term
                    spot = PAD + n_bytes + slot - tap
                    corr = corr + wide_ref[c, spot : spot + 1, :] * weight
                else:
                    here = here + term
            if slot < KCONV - 1:
                here = here + before * keep_ref[0:toks, :]
                corr = corr * keep_ref[toks : toks + 1, :]
            short = here.astype(BF16)
            short_ref[:, at : at + 128] = short
            short = short.astype(F32)
            squares = squares + short * short
            gain = gain_ref[:, at : at + 128]
            u_ref[0:toks, at : at + 128] = (short * gain).astype(BF16)
            row = iota((EDGE, 128), 0)
            u_ref[toks:, at : at + 128] = jnp.where(row == 0, corr * gain, 0.0).astype(BF16)
            r, o = at // part, at % part
            fold_ref[r : r + 1, o : o + 128] = short[0:1]
            fold_ref[8 + r : 9 + r, o : o + 128] = corr
        for copy in weights[slot]:
            copy.wait()
        span = slice(slot * byte_dim, (slot + 1) * byte_dim)
        got = jnp.dot(u_ref[:, span], w_ref[span, :], preferred_element_type=F32)
        if slot == 0:
            acc_ref[...] = got
        else:
            acc_ref[...] += got
    rs = lax.rsqrt(jnp.sum(squares, axis=1, keepdims=True) * (1.0 / width) + 1e-06)
    out_ref[0:toks, :] = (acc_ref[0:toks, 0 : 2 * kv] * rs).astype(BF16)
    lat_ref[...] = (acc_ref[0:toks, 2 * kv :] * rs).astype(BF16)
    edge_ref[...] = acc_ref[0:8, :]
    row = iota((EDGE, 2 * kv), 0)
    low = jnp.concatenate(
        [acc_ref[toks : toks + 1, 2 * kv :], jnp.zeros((1, 2 * kv - rank), F32)], axis=1
    )
    sums = jnp.where(row == 0, acc_ref[0:1, 0 : 2 * kv], 0.0)
    sums = jnp.where(row == 1, acc_ref[toks : toks + 1, 0 : 2 * kv], sums)
    out_ref[toks : toks + EDGE, :] = jnp.where(row == 2, low, sums).astype(BF16)
    out_ref[toks + EDGE : toks + 2 * EDGE, 0:part] = fold_ref[...].astype(BF16)


def plan_kernel(n_seq, rows, me_ref, lens_ref, dest_ref, bias_ref, pick_ref, fill_ref):
    toks, keys = bias_ref.shape
    me = me_ref[0]
    pos = me * toks + iota((toks, 128), 0)

    def doc(d, carry):
        first, begin = carry
        return first + lens_ref[d], jnp.where(pos >= first, first, begin)

    _, begin = lax.fori_loop(
        0, lens_ref.shape[0], doc, (jnp.int32(0), jnp.zeros((toks, 128), jnp.int32))
    )
    for at in range(0, keys, 128):
        key = (me - BACK) * toks + at + iota((toks, 128), 1)
        bias_ref[:, at : at + 128] = jnp.where((key >= begin) & (key <= pos), 0.0, -1e30)
    lane = iota((8, toks), 1)
    panel = lane // PANEL
    dest = jnp.full((8, toks), -1, jnp.int32)
    for p in range(toks // PANEL):
        dest = jnp.where(panel == p, dest_ref[p], dest)
    rank = jnp.zeros((8, toks), jnp.int32)
    for p in range(toks // PANEL):
        rank = rank + jnp.where((panel > p) & (dest == dest_ref[p]), 1, 0)
    place = (dest ^ me) * rows + rank * PANEL + lane % PANEL
    hit = jnp.where(iota((n_seq * rows, toks), 0) == place[0:1], 1.0, 0.0)
    pick_ref[...] = hit.astype(BF16)
    used = jnp.sum(hit, axis=1, keepdims=True)
    fill_ref[...] = jnp.broadcast_to((1.0 - used) * MARK, fill_ref.shape)


def attend_kernel(
    n_seq, rows, merged, lat_ref, edge_ref, own_ref, one_ref, two_ref, bias_ref, pick_ref, fill_ref,
    wq_ref, short_ref, *refs,
):
    n_out = 1 if merged else n_seq
    block_refs = refs[:n_out]
    k_ref, v_ref, query_ref, corr_ref = refs[n_out:]
    toks, hd = lat_ref.shape
    kvh = k_ref.shape[0]
    kv = kvh * hd
    width = corr_ref.shape[1]
    part = width // 8
    heads = wq_ref.shape[1] // hd
    keys = bias_ref.shape[1]
    step = pl.program_id(0)

    @pl.when(step == 0)
    def _():
        def root(first):
            total = jnp.sum(jnp.sum(first * first, axis=1, keepdims=True), axis=0, keepdims=True)
            return lax.rsqrt(total * (1.0 / width) + 1e-06)

        fold = slice(toks + EDGE, toks + 2 * EDGE)
        sums = slice(toks, toks + EDGE)
        own_fold = own_ref[fold, 0:part].astype(F32)
        one_fold = one_ref[fold, 0:part].astype(F32)
        two_fold = two_ref[fold, 0:part].astype(F32)
        one_sums = one_ref[sums, :].astype(F32)
        two_sums = two_ref[sums, :].astype(F32)
        scale = root((own_fold[0:8] + one_fold[8:16]).astype(BF16).astype(F32))
        own_kv = scale * (edge_ref[0:1, 0 : 2 * kv] + one_sums[1:2])
        own_lat = scale * (edge_ref[0:1, 2 * kv :] + one_sums[2:3, 0:hd])
        scale = root((one_fold[0:8] + two_fold[8:16]).astype(BF16).astype(F32))
        one_kv = scale * (one_sums[0:1] + two_sums[1:2])
        row = iota((EDGE, 2 * kv), 0)
        tops = [
            two_ref[0:EDGE, :],
            jnp.where(row == 0, one_kv, one_ref[0:EDGE, :].astype(F32)).astype(BF16),
            jnp.where(row == 0, own_kv, own_ref[0:EDGE, :].astype(F32)).astype(BF16),
        ]
        for b, ref in enumerate((two_ref, one_ref, own_ref)):
            at = b * toks
            for g in range(kvh):
                cols = slice(g * hd, (g + 1) * hd)
                k_ref[g, at : at + EDGE, :] = tops[b][:, cols]
                k_ref[g, at + EDGE : at + toks, :] = ref[EDGE:toks, cols]
                cols = slice(kv + g * hd, kv + (g + 1) * hd)
                v_ref[g, at : at + EDGE, 0:hd] = tops[b][:, cols]
                v_ref[g, at + EDGE : at + toks, 0:hd] = ref[EDGE:toks, cols]
                v_ref[g, at : at + toks, hd:] = jnp.ones((toks, hd), BF16)
        row = iota((EDGE, hd), 0)
        query_ref[0:EDGE, :] = jnp.where(row == 0, own_lat, lat_ref[0:EDGE, :].astype(F32)).astype(BF16)
        query_ref[EDGE:, :] = lat_ref[EDGE:, :]
        for c in range(8):
            corr_ref[:, c * part : (c + 1) * part] = one_fold[8 + c : 9 + c]

    log_scale = math.log2(math.e) / math.sqrt(hd)
    group = step // (pl.num_programs(0) // kvh)
    query = (jnp.dot(query_ref[...], wq_ref[...], preferred_element_type=F32) * log_scale).astype(BF16)
    query = jnp.concatenate([query[:, h * hd : (h + 1) * hd] for h in range(heads)], axis=0)
    scores = lax.dot_general(
        query, k_ref[group], (((1,), (1,)), ((), ())), preferred_element_type=F32
    )
    scores = scores.reshape(heads, toks, keys) + bias_ref[...][None]
    top = jnp.max(scores, axis=2, keepdims=True)
    probs = jnp.exp2(scores - top).astype(BF16).reshape(heads * toks, keys)
    mixed = jnp.dot(probs, v_ref[group], preferred_element_type=F32)
    mixed = mixed[:, 0:hd] / mixed[:, hd:]
    mixed = jnp.concatenate([mixed[h * toks : (h + 1) * toks] for h in range(heads)], axis=1)
    wide = heads * hd
    cols = pl.ds(pl.multiple_of(step * wide, wide), wide)
    short = short_ref[...].astype(F32)
    whole = (short[0:EDGE] + corr_ref[:, cols]).astype(BF16).astype(F32)
    first = jnp.where(iota((EDGE, wide), 0) == 0, whole, short[0:EDGE])
    layer = (mixed + jnp.concatenate([first, short[EDGE:]], axis=0)).astype(BF16)
    placed = jnp.dot(pick_ref[...], layer, preferred_element_type=F32)
    placed = (placed + fill_ref[:, 0:1]).astype(BF16)
    if merged:
        block_refs[0][...] = placed
    else:
        for k in range(n_seq):
            block_refs[k][...] = placed[k * rows : (k + 1) * rows]


def gather_kernel(order, rows, pans, me_ref, *refs):
    n_out = 3
    block_refs, (acc_ref, last_ref, sel_ref) = refs[:-n_out], refs[-n_out:]
    toks = acc_ref.shape[0]
    n_seq = len(order)
    blocks = [r[...] for r in block_refs]
    got = blocks[0] if len(blocks) == 1 else jnp.concatenate(blocks, axis=0)
    step = pl.program_id(0)
    me = me_ref[0]

    @pl.when(step == 0)
    def _():
        n_pad = max(16, n_seq)
        used = jnp.where(got[:, 0:128].astype(F32) < 0.5 * MARK, 1.0, 0.0).astype(BF16)
        member = iota((n_pad, got.shape[0]), 0) == iota((n_pad, got.shape[0]), 1) // rows
        count = jnp.dot(jnp.where(member, 1.0, 0.0).astype(BF16), used, preferred_element_type=F32)
        rest = pans * PANEL - jnp.sum(count, axis=0, keepdims=True)
        place = iota((n_pad, 128), 0)
        count = jnp.where(place == n_seq - 1, rest, count)
        source = jnp.full((n_pad, 128), n_seq, jnp.int32)
        for q in range(n_seq):
            source = jnp.where(place == q, me ^ order[q], source)
        offset = jnp.zeros((n_pad, 128), F32)
        for q in range(n_seq):
            offset = offset + jnp.where(source > (me ^ order[q]), count[q : q + 1], 0.0)

        def targets(parts, wide):
            lane = iota((1, wide), 1)
            within = (lane % rows).astype(F32)
            target = jnp.full((1, wide), -1.0, F32)
            for i, q in enumerate(parts):
                valid = (lane // rows == i) & (within < count[q : q + 1, 0:1])
                target = jnp.where(valid, offset[q : q + 1, 0:1] + within, target)
            row = iota((toks, wide), 0).astype(F32)
            return jnp.where(row == target, 1.0, 0.0).astype(BF16)

        sel_ref[...] = targets(range(n_seq - 1), got.shape[0])
        last_ref[...] = targets([n_seq - 1], last_ref.shape[1])

    acc_ref[...] = jnp.dot(sel_ref[...], got, preferred_element_type=F32)


def finish_kernel(acc_ref, last_ref, block_ref, out_ref):
    out_ref[...] = (
        acc_ref[...] + jnp.dot(last_ref[...], block_ref[...], preferred_element_type=F32)
    ).astype(BF16)


def smem():
    return pl.BlockSpec(memory_space=pltpu.SMEM)


def vmem():
    return pl.BlockSpec(memory_space=pltpu.VMEM)


def hbm():
    return pl.BlockSpec(memory_space=pltpu.HBM)


def whole_block(shape):
    return pl.BlockSpec(shape, lambda i: (0,) * len(shape))


def column_block(rows, cols):
    return pl.BlockSpec((rows, cols), lambda i: (0, i))


def params(limit=VMEM_BYTES):
    return pltpu.CompilerParams(vmem_limit_bytes=limit)


def per_device(
    byte_embed, conv_taps, norm_gain, w_qdown, w_qup, w_key, w_value, doc_lengths, panel_dest
):
    n_seq = lax.axis_size("seq")
    me = lax.axis_index("seq").astype(jnp.int32).reshape(1)
    n_bytes, byte_dim = byte_embed.shape
    toks = n_bytes // SHORTEN
    width = SHORTEN * byte_dim
    hd = width // H
    kv = w_key.shape[1]
    kvh = kv // hd
    rank = w_qdown.shape[1]
    pans = toks // PANEL
    slots = (2 * pans + n_seq - 1) // n_seq
    rows = slots * PANEL
    merged = rows % 16 != 0
    keys = (BACK + 1) * toks
    held_rows = toks + 2 * EDGE

    held, short, latent, edge = pl.pallas_call(
        project_kernel,
        out_shape=[
            jax.ShapeDtypeStruct((held_rows, 2 * kv), BF16),
            jax.ShapeDtypeStruct((toks, width), BF16),
            jax.ShapeDtypeStruct((toks, rank), BF16),
            jax.ShapeDtypeStruct((8, 2 * kv + rank), F32),
        ],
        in_specs=[smem()] + [hbm()] * 7,
        out_specs=[vmem()] * 4,
        scratch_shapes=[
            pltpu.SMEM(doc_lengths.shape, jnp.int32),
            pltpu.VMEM((n_bytes, byte_dim), BF16),
            pltpu.VMEM((KCONV, byte_dim), F32),
            pltpu.VMEM((1, width), F32),
            pltpu.VMEM((width, 2 * kv + rank), BF16),
            pltpu.SemaphoreType.DMA((7,)),
            pltpu.SemaphoreType.DMA((SHORTEN, 3)),
            pltpu.VMEM((byte_dim // 128, n_bytes + 2 * PAD, 128), F32),
            pltpu.VMEM((toks + 8, 128), F32),
            pltpu.VMEM((toks + EDGE, width), BF16),
            pltpu.VMEM((toks + EDGE, 2 * kv + rank), F32),
            pltpu.VMEM((16, width // 8), F32),
        ],
        compiler_params=params(ALL_VMEM),
        name="project",
    )(me, doc_lengths, byte_embed, conv_taps, norm_gain.reshape(1, width), w_key, w_value, w_qdown)

    behind = [
        lax.ppermute(held, "seq", [(i, i + by) for i in range(n_seq - by)])
        for by in range(1, BACK + 1)
    ]

    bias, pick, fill = pl.pallas_call(
        functools.partial(plan_kernel, n_seq, rows),
        out_shape=[
            jax.ShapeDtypeStruct((toks, keys), F32),
            jax.ShapeDtypeStruct((n_seq * rows, toks), BF16),
            jax.ShapeDtypeStruct((n_seq * rows, 128), F32),
        ],
        in_specs=[smem()] * 3,
        out_specs=[vmem()] * 3,
        compiler_params=params(),
        name="plan",
    )(me, doc_lengths, panel_dest)

    heads = min(4, H // kvh)
    wide = heads * hd
    block_rows = n_seq * rows if merged else rows
    n_out = 1 if merged else n_seq
    blocks = pl.pallas_call(
        functools.partial(attend_kernel, n_seq, rows, merged),
        grid=(H // heads,),
        out_shape=[jax.ShapeDtypeStruct((block_rows, width), BF16)] * n_out,
        in_specs=[
            whole_block(latent.shape),
            whole_block(edge.shape),
            whole_block(held.shape),
            whole_block(held.shape),
            whole_block(held.shape),
            whole_block(bias.shape),
            whole_block(pick.shape),
            whole_block(fill.shape),
            column_block(rank, wide),
            column_block(toks, wide),
        ],
        out_specs=[column_block(block_rows, wide)] * n_out,
        scratch_shapes=[
            pltpu.VMEM((kvh, keys, hd), BF16),
            pltpu.VMEM((kvh, keys, 2 * hd), BF16),
            pltpu.VMEM((toks, rank), BF16),
            pltpu.VMEM((1, width), F32),
        ],
        compiler_params=params(),
        name="attend",
    )(latent, edge, held, behind[0], behind[1], bias, pick, fill, w_qup, short)
    if merged:
        blocks = [blocks[0][k * rows : (k + 1) * rows] for k in range(n_seq)]

    order = [0] + list(range(n_seq // 2, n_seq)) + list(range(1, n_seq // 2))
    got = [blocks[0]] + [
        lax.ppermute(blocks[k], "seq", [(i, i ^ k) for i in range(n_seq)]) for k in order[1:]
    ]
    last_at = n_seq // 2
    order = order[:last_at] + order[last_at + 1 :] + [order[last_at]]
    got = got[:last_at] + got[last_at + 1 :] + [got[last_at]]
    last = got.pop()
    if merged:
        got = [jnp.concatenate(got, axis=0)]
        last = jnp.pad(last, ((0, -rows % 16), (0, 0)))
    out_cols = width // 4
    n_rows = (n_seq - 1) * rows
    acc, sel = pl.pallas_call(
        functools.partial(gather_kernel, order, rows, pans),
        grid=(4,),
        out_shape=[
            jax.ShapeDtypeStruct((toks, width), F32),
            jax.ShapeDtypeStruct((toks, last.shape[0]), BF16),
        ],
        in_specs=[smem()] + [column_block(g.shape[0], out_cols) for g in got],
        out_specs=[column_block(toks, out_cols), whole_block((toks, last.shape[0]))],
        scratch_shapes=[pltpu.VMEM((toks, n_rows), BF16)],
        compiler_params=params(),
        name="gather",
    )(me, *got)
    return pl.pallas_call(
        finish_kernel,
        grid=(4,),
        out_shape=jax.ShapeDtypeStruct((toks, width), BF16),
        in_specs=[
            column_block(toks, out_cols),
            whole_block(sel.shape),
            column_block(last.shape[0], out_cols),
        ],
        out_specs=column_block(toks, out_cols),
        compiler_params=params(),
        name="finish",
    )(acc, sel, last)


def solution(mesh):
    in_specs = (P(("dp", "seq"), None), P(), P(), P(), P(), P(), P(), P("dp"), P(("dp", "seq")))
    out_specs = P(("dp", "seq"), None)
    return jax.shard_map(
        per_device, mesh=mesh, in_specs=in_specs, out_specs=out_specs, check_vma=False
    )
```

```python
import functools
import math

import jax
import jax.numpy as jnp
from jax import lax
from jax.experimental import pallas as pl
from jax.experimental.pallas import tpu as pltpu
from jax.sharding import PartitionSpec as P

H = 32
SHORTEN = 4
KCONV = 4
PANEL = 4
BACK = 2
PAD = 8
EDGE = 16
MARK = 2.0**120
BATCH = 8
MIB = 1024 * 1024
F32 = jnp.float32
BF16 = jnp.bfloat16


def iota(shape, dim):
    return lax.broadcasted_iota(jnp.int32, shape, dim)


def project_kernel(
    lens_hbm, x_hbm, taps_hbm, gain_hbm, wk_hbm, wv_hbm, wd_hbm,
    out_ref, short_ref, lat_ref, edge_ref,
    lens_ref, x_ref, taps_ref, gain_ref, w_ref, sems, wsems, wide_ref, keep_ref, u_ref, acc_ref, fold_ref,
):
    n_bytes, byte_dim = x_ref.shape
    toks, width = short_ref.shape
    kv = wk_hbm.shape[1]
    rank = wd_hbm.shape[1]
    me = lax.axis_index("seq")
    pieces = 2
    some = n_bytes // pieces
    large = [
        pltpu.make_async_copy(
            x_hbm.at[pl.ds(i * some, some)], x_ref.at[pl.ds(i * some, some)], sems.at[3 + i]
        )
        for i in range(pieces)
    ]
    small = [
        pltpu.make_async_copy(lens_hbm, lens_ref, sems.at[0]),
        pltpu.make_async_copy(taps_hbm, taps_ref, sems.at[1]),
        pltpu.make_async_copy(gain_hbm, gain_ref, sems.at[2]),
    ]
    weights = []
    for i in range(SHORTEN):
        at = pl.ds(i * byte_dim, byte_dim)
        weights.append(
            [
                pltpu.make_async_copy(wk_hbm.at[at], w_ref.at[at, pl.ds(0, kv)], wsems.at[i, 0]),
                pltpu.make_async_copy(wv_hbm.at[at], w_ref.at[at, pl.ds(kv, kv)], wsems.at[i, 1]),
                pltpu.make_async_copy(wd_hbm.at[at], w_ref.at[at, pl.ds(2 * kv, rank)], wsems.at[i, 2]),
            ]
        )
    for copy in small + large:
        copy.start()
    for c in range(byte_dim // 128):
        wide_ref[c, 0:PAD, :] = jnp.zeros((PAD, 128), F32)
        wide_ref[c, PAD + n_bytes :, :] = jnp.zeros((PAD, 128), F32)
    u_ref[toks:, :] = jnp.zeros((EDGE, width), BF16)
    for copy in small:
        copy.wait()
    token = me * toks + iota((toks + 8, 128), 0)

    def doc(d, carry):
        first, keep = carry
        return first + lens_ref[d], jnp.where(token == first, 0.0, keep)

    _, keep = lax.fori_loop(
        0, lens_ref.shape[0], doc, (jnp.int32(0), jnp.ones((toks + 8, 128), F32))
    )
    keep_ref[...] = keep
    for i, copy in enumerate(large):
        copy.wait()
        if i == 0:
            for group in weights:
                for one in group:
                    one.start()
        for c in range(byte_dim // 128):
            wide_ref[c, PAD + i * some : PAD + (i + 1) * some, :] = x_ref[
                i * some : (i + 1) * some, c * 128 : (c + 1) * 128
            ].astype(F32)

    part = width // 8
    squares = [jnp.zeros((toks, 128), F32)]

    def conv(slot):
        for c in range(byte_dim // 128):
            cols = slice(c * 128, (c + 1) * 128)
            at = slot * byte_dim + c * 128
            here = jnp.zeros((toks, 128), F32)
            before = jnp.zeros((toks, 128), F32)
            corr = jnp.zeros((1, 128), F32)
            for tap in range(KCONV):
                weight = taps_ref[tap : tap + 1, cols]
                term = wide_ref[c, pl.ds(PAD + slot - tap, toks, stride=SHORTEN), :] * weight
                if tap > slot:
                    before = before + term
                    spot = PAD + n_bytes + slot - tap
                    corr = corr + wide_ref[c, spot : spot + 1, :] * weight
                else:
                    here = here + term
            if slot < KCONV - 1:
                here = here + before * keep_ref[0:toks, :]
                corr = corr * keep_ref[toks : toks + 1, :]
            short = here.astype(BF16)
            short_ref[:, at : at + 128] = short
            short = short.astype(F32)
            squares[0] = squares[0] + short * short
            gain = gain_ref[:, at : at + 128]
            u_ref[0:toks, at : at + 128] = (short * gain).astype(BF16)
            row = iota((EDGE, 128), 0)
            u_ref[toks:, at : at + 128] = jnp.where(row == 0, corr * gain, 0.0).astype(BF16)
            r, o = at // part, at % part
            fold_ref[r : r + 1, o : o + 128] = short[0:1]
            fold_ref[8 + r : 9 + r, o : o + 128] = corr

    def project(slot):
        for copy in weights[slot]:
            copy.wait()
        span = slice(slot * byte_dim, (slot + 1) * byte_dim)
        got = jnp.dot(u_ref[:, span], w_ref[span, :], preferred_element_type=F32)
        if slot == 0:
            acc_ref[...] = got
        else:
            acc_ref[...] += got

    conv(0)
    for slot in range(1, SHORTEN):
        conv(slot)
        project(slot - 1)
    project(SHORTEN - 1)
    rs = lax.rsqrt(jnp.sum(squares[0], axis=1, keepdims=True) * (1.0 / width) + 1e-06)
    out_ref[0:toks, :] = (acc_ref[0:toks, 0 : 2 * kv] * rs).astype(BF16)
    lat_ref[...] = (acc_ref[0:toks, 2 * kv :] * rs).astype(BF16)
    edge_ref[...] = acc_ref[0:8, :]
    row = iota((EDGE, 2 * kv), 0)
    low = jnp.concatenate(
        [acc_ref[toks : toks + 1, 2 * kv :], jnp.zeros((1, 2 * kv - rank), F32)], axis=1
    )
    sums = jnp.where(row == 0, acc_ref[0:1, 0 : 2 * kv], 0.0)
    sums = jnp.where(row == 1, acc_ref[toks : toks + 1, 0 : 2 * kv], sums)
    out_ref[toks : toks + EDGE, :] = jnp.where(row == 2, low, sums).astype(BF16)
    out_ref[toks + EDGE : toks + 2 * EDGE, 0:part] = fold_ref[...].astype(BF16)


def plan_kernel(n_seq, rows, lens_ref, dest_ref, bias_ref, pick_ref):
    toks, keys = bias_ref.shape
    me = lax.axis_index("seq")
    pos = me * toks + iota((toks, 128), 0)

    def doc(d, carry):
        first, begin = carry
        return first + lens_ref[d], jnp.where(pos >= first, first, begin)

    _, begin = lax.fori_loop(
        0, lens_ref.shape[0], doc, (jnp.int32(0), jnp.zeros((toks, 128), jnp.int32))
    )
    for at in range(0, keys, 128):
        key = (me - BACK) * toks + at + iota((toks, 128), 1)
        bias_ref[:, at : at + 128] = jnp.where((key >= begin) & (key <= pos), 0.0, -1e30)
    lane = iota((8, toks), 1)
    panel = lane // PANEL
    dest = jnp.full((8, toks), -1, jnp.int32)
    for p in range(toks // PANEL):
        dest = jnp.where(panel == p, dest_ref[p], dest)
    rank = jnp.zeros((8, toks), jnp.int32)
    for p in range(toks // PANEL):
        rank = rank + jnp.where((panel > p) & (dest == dest_ref[p]), 1, 0)
    place = (dest ^ me) * rows + rank * PANEL + lane % PANEL
    row = iota((n_seq * rows, toks), 0)
    pick_ref[...] = jnp.where(row == place[0:1], 1.0, 0.0).astype(BF16)


def put_blocks(pick, layer, refs):
    empty = (1.0 - jnp.sum(pick.astype(F32), axis=1, keepdims=True)) * MARK
    placed = (jnp.dot(pick, layer, preferred_element_type=F32) + empty).astype(BF16)
    rows = refs[0].shape[0]
    for k, ref in enumerate(refs):
        ref[...] = placed[k * rows : (k + 1) * rows]


def attend_kernel(half, batch, lat_ref, edge_ref, own_ref, one_ref, two_ref, bias_ref, pick_ref, wq_ref, short_ref, *refs):
    refs, (k_ref, v_ref, query_ref, corr_ref, layer_ref) = refs[:-5], refs[-5:]
    if half == 0:
        cross_refs, out_layer_ref = refs[:-1], refs[-1]
    else:
        past_ref, refs = refs[0], refs[1:]
        cross_refs, near_refs = refs[: len(refs) // 2], refs[len(refs) // 2 :]
    toks, hd = lat_ref.shape
    wide = layer_ref.shape[1]
    heads = wide // hd
    kv = own_ref.shape[1] // 2
    part = own_ref.shape[1]
    width = 8 * part
    keys = bias_ref.shape[1]

    def root(first):
        total = jnp.sum(jnp.sum(first * first, axis=1, keepdims=True), axis=0, keepdims=True)
        return lax.rsqrt(total * (1.0 / width) + 1e-06)

    fold = slice(toks + EDGE, toks + 2 * EDGE)
    sums = slice(toks, toks + EDGE)
    own_fold = own_ref[fold, :].astype(F32)
    one_fold = one_ref[fold, :].astype(F32)
    two_fold = two_ref[fold, :].astype(F32)
    one_sums = one_ref[sums, :].astype(F32)
    two_sums = two_ref[sums, :].astype(F32)
    scale = root((own_fold[0:8] + one_fold[8:16]).astype(BF16).astype(F32))
    own_kv = scale * (edge_ref[0:1, 0 : 2 * kv] + one_sums[1:2])
    own_lat = scale * (edge_ref[0:1, 2 * kv :] + one_sums[2:3, 0:hd])
    scale = root((one_fold[0:8] + two_fold[8:16]).astype(BF16).astype(F32))
    one_kv = scale * (one_sums[0:1] + two_sums[1:2])
    row = iota((EDGE, 2 * kv), 0)
    tops = [
        two_ref[0:EDGE, :],
        jnp.where(row == 0, one_kv, one_ref[0:EDGE, :].astype(F32)).astype(BF16),
        jnp.where(row == 0, own_kv, own_ref[0:EDGE, :].astype(F32)).astype(BF16),
    ]
    k_cols = slice(half * hd, (half + 1) * hd)
    v_cols = slice(kv + half * hd, kv + (half + 1) * hd)
    for b, ref in enumerate((two_ref, one_ref, own_ref)):
        at = b * toks
        k_ref[at : at + EDGE, :] = tops[b][:, k_cols]
        k_ref[at + EDGE : at + toks, :] = ref[EDGE:toks, k_cols]
        v_ref[at : at + EDGE, 0:hd] = tops[b][:, v_cols]
        v_ref[at + EDGE : at + toks, 0:hd] = ref[EDGE:toks, v_cols]
        v_ref[at : at + toks, hd:] = jnp.ones((toks, hd), BF16)
    row = iota((EDGE, hd), 0)
    query_ref[0:EDGE, :] = jnp.where(row == 0, own_lat, lat_ref[0:EDGE, :].astype(F32)).astype(BF16)
    query_ref[EDGE:, :] = lat_ref[EDGE:, :]
    for c in range(wide // part):
        at = half * (wide // part) + c
        corr_ref[:, c * part : (c + 1) * part] = one_fold[8 + at : 9 + at]

    log_scale = math.log2(math.e) / math.sqrt(hd)
    wq = wq_ref[:, half * wide : (half + 1) * wide]
    query = (jnp.dot(query_ref[...], wq, preferred_element_type=F32) * log_scale).astype(BF16)
    key_all, value_all = k_ref[...], v_ref[...]
    for at in range(0, heads, batch):
        part_q = [query[:, h * hd : (h + 1) * hd] for h in range(at, at + batch)]
        scores = lax.dot_general(
            jnp.concatenate(part_q, axis=0), key_all, (((1,), (1,)), ((), ())), preferred_element_type=F32
        )
        scores = scores.reshape(batch, toks, keys) + bias_ref[...][None]
        top = jnp.max(scores, axis=2, keepdims=True)
        probs = jnp.exp2(scores - top).astype(BF16).reshape(batch * toks, keys)
        mixed = jnp.dot(probs, value_all, preferred_element_type=F32)
        mixed = mixed[:, 0:hd] / mixed[:, hd:]
        for h in range(batch):
            cols = slice((at + h) * hd, (at + h + 1) * hd)
            short = short_ref[:, half * wide + (at + h) * hd : half * wide + (at + h + 1) * hd].astype(F32)
            whole = (short[0:8] + corr_ref[:, cols]).astype(BF16).astype(F32)
            first = jnp.where(iota((8, hd), 0) == 0, whole, short[0:8])
            short = jnp.concatenate([first, short[8:]], axis=0)
            layer_ref[:, cols] = (mixed[h * toks : (h + 1) * toks] + short).astype(BF16)
    middle = pick_ref.shape[0] // 2
    put_blocks(pick_ref[middle:, :], layer_ref[...], cross_refs)
    if half == 0:
        out_layer_ref[...] = layer_ref[...]
    else:
        layer = jnp.concatenate([past_ref[...], layer_ref[...]], axis=1)
        put_blocks(pick_ref[0:middle, :], layer, near_refs)


def first_kernel(n_seq, rows, *refs):
    block_refs, (out_ref, sel_ref, pick_ref) = refs[:-3], refs[-3:]
    toks = out_ref.shape[0]
    got = jnp.concatenate([r[...] for r in block_refs], axis=0)
    me = lax.axis_index("seq")

    @pl.when(pl.program_id(0) == 0)
    def _():
        n_pad = max(16, n_seq)
        n_rows = got.shape[0]
        used = jnp.where(got[:, 0:128].astype(F32) < 0.5 * MARK, 1.0, 0.0).astype(BF16)
        member = iota((n_pad, n_rows), 0) == iota((n_pad, n_rows), 1) // rows
        count = jnp.dot(jnp.where(member, 1.0, 0.0).astype(BF16), used, preferred_element_type=F32)
        source = me ^ iota((n_pad, 128), 0)
        offset = jnp.zeros((n_pad, 128), F32)
        for q in range(n_seq):
            offset = offset + jnp.where(source > (me ^ q), count[q : q + 1], 0.0)
        lane = iota((1, n_rows), 1)
        within = (lane % rows).astype(F32)
        target = jnp.full((1, n_rows), -1.0, F32)
        for q in range(n_seq):
            valid = (lane // rows == q) & (within < count[q : q + 1, 0:1])
            target = jnp.where(valid, offset[q : q + 1, 0:1] + within, target)
        row = iota((toks, n_rows), 0).astype(F32)
        pick_ref[...] = jnp.where(row == target, 1.0, 0.0).astype(BF16)
        sel_ref[...] = pick_ref[...]

    out_ref[...] = jnp.dot(pick_ref[...], got, preferred_element_type=F32).astype(BF16)


def second_kernel(sel_ref, *refs):
    block_refs, out_ref = refs[:-2], refs[-1]
    got = jnp.concatenate([r[...] for r in block_refs], axis=0)
    out_ref[...] = jnp.dot(sel_ref[...], got, preferred_element_type=F32).astype(BF16)


def swap(array, by, size):
    return lax.ppermute(array, "seq", [(i, i ^ by) for i in range(size)])


def smem():
    return pl.BlockSpec(memory_space=pltpu.SMEM)


def vmem():
    return pl.BlockSpec(memory_space=pltpu.VMEM)


def hbm():
    return pl.BlockSpec(memory_space=pltpu.HBM)


def in_hbm(array):
    return pltpu.with_memory_space_constraint(array, pltpu.HBM)


def whole_block(shape):
    return pl.BlockSpec(shape, lambda i: (0,) * len(shape))


def column_block(rows, cols):
    return pl.BlockSpec((rows, cols), lambda i: (0, i))


def params(limit=32 * MIB):
    return pltpu.CompilerParams(vmem_limit_bytes=limit)


def per_device(
    byte_embed, conv_taps, norm_gain, w_qdown, w_qup, w_key, w_value, doc_lengths, panel_dest
):
    n_seq = lax.axis_size("seq")
    n_bytes, byte_dim = byte_embed.shape
    toks = n_bytes // SHORTEN
    width = SHORTEN * byte_dim
    hd = width // H
    kv = w_key.shape[1]
    kvh = kv // hd
    rank = w_qdown.shape[1]
    pans = toks // PANEL
    slots = (2 * pans + n_seq - 1) // n_seq
    rows = slots * PANEL
    merged = rows % 16 != 0
    keys = (BACK + 1) * toks
    held_rows = toks + 2 * EDGE

    held, short, latent, edge = pl.pallas_call(
        project_kernel,
        out_shape=[
            pltpu.VMEM((held_rows, 2 * kv), BF16),
            pltpu.VMEM((toks, width), BF16),
            pltpu.VMEM((toks, rank), BF16),
            pltpu.VMEM((8, 2 * kv + rank), F32),
        ],
        in_specs=[hbm()] * 7,
        out_specs=[vmem()] * 4,
        scratch_shapes=[
            pltpu.SMEM(doc_lengths.shape, jnp.int32),
            pltpu.VMEM((n_bytes, byte_dim), BF16),
            pltpu.VMEM((KCONV, byte_dim), F32),
            pltpu.VMEM((1, width), F32),
            pltpu.VMEM((width, 2 * kv + rank), BF16),
            pltpu.SemaphoreType.DMA((5,)),
            pltpu.SemaphoreType.DMA((SHORTEN, 3)),
            pltpu.VMEM((byte_dim // 128, n_bytes + 2 * PAD, 128), F32),
            pltpu.VMEM((toks + 8, 128), F32),
            pltpu.VMEM((toks + EDGE, width), BF16),
            pltpu.VMEM((toks + EDGE, 2 * kv + rank), F32),
            pltpu.VMEM((16, width // 8), F32),
        ],
        compiler_params=params(24 * MIB),
        name="project",
    )(
        *[
            in_hbm(a)
            for a in (
                doc_lengths, byte_embed, conv_taps, norm_gain.reshape(1, width), w_key, w_value, w_qdown
            )
        ]
    )

    behind = [
        lax.ppermute(held, "seq", [(i, i + by) for i in range(n_seq - by)])
        for by in range(1, BACK + 1)
    ]

    bias, pick = pl.pallas_call(
        functools.partial(plan_kernel, n_seq, rows),
        out_shape=[
            pltpu.VMEM((toks, keys), F32),
            pltpu.VMEM((n_seq * rows, toks), BF16),
        ],
        in_specs=[smem()] * 2,
        out_specs=[vmem()] * 2,
        compiler_params=params(),
        name="plan",
    )(doc_lengths, panel_dest)

    middle = n_seq // 2
    span = width // kvh
    batch = BATCH
    n_out, out_rows = (1, middle * rows) if merged else (middle, rows)

    def split(blocks):
        if merged:
            return [blocks[0][k * rows : (k + 1) * rows] for k in range(middle)]
        return list(blocks)

    def attend(half, more):
        cross = [pltpu.VMEM((out_rows, span), BF16)] * n_out
        near = [pltpu.VMEM((out_rows, width), BF16)] * n_out
        outs = cross + ([pltpu.VMEM((toks, span), BF16)] if half == 0 else near)
        operands = [latent, edge, held, *behind, bias, pick, w_qup, short, *more]
        return pl.pallas_call(
            functools.partial(attend_kernel, half, batch),
            out_shape=outs,
            in_specs=[vmem()] * len(operands),
            out_specs=[vmem()] * len(outs),
            scratch_shapes=[
                pltpu.VMEM((keys, hd), BF16),
                pltpu.VMEM((keys, 2 * hd), BF16),
                pltpu.VMEM((toks, rank), BF16),
                pltpu.VMEM((1, span), F32),
                pltpu.VMEM((toks, span), BF16),
            ],
            compiler_params=params(),
            name=f"attend_half_{half}",
        )(*operands)

    *first_cross, layer = attend(0, [])
    got_first = [swap(x, middle + k, n_seq) for k, x in enumerate(split(first_cross))]
    outs = attend(1, [layer])
    got_second = [swap(x, middle + k, n_seq) for k, x in enumerate(split(outs[:n_out]))]
    near = split(outs[n_out:])
    got_near = [near[0]] + [swap(near[k], k, n_seq) for k in range(1, middle)]
    if merged:
        got_first, got_second, got_near = (
            [jnp.concatenate(g, axis=0)] for g in (got_first, got_second, got_near)
        )

    steps = 4
    cols = span // steps

    def columns(arrays, start):
        return [pl.BlockSpec((a.shape[0], cols), lambda i: (0, start + i)) for a in arrays]

    out, sel = pl.pallas_call(
        functools.partial(first_kernel, n_seq, rows),
        grid=(steps,),
        out_shape=[
            jax.ShapeDtypeStruct((toks, width), BF16),
            jax.ShapeDtypeStruct((toks, n_seq * rows), BF16),
        ],
        in_specs=columns(got_near, 0) + columns(got_first, 0),
        out_specs=[
            pl.BlockSpec((toks, cols), lambda i: (0, i)),
            whole_block((toks, n_seq * rows)),
        ],
        scratch_shapes=[pltpu.VMEM((toks, n_seq * rows), BF16)],
        compiler_params=params(),
        name="place_first",
    )(*got_near, *got_first)
    operands = [sel, *got_near, *got_second, out]
    return pl.pallas_call(
        second_kernel,
        grid=(steps,),
        out_shape=jax.ShapeDtypeStruct((toks, width), BF16),
        in_specs=[whole_block(sel.shape)]
        + columns(got_near, steps)
        + columns(got_second, 0)
        + [pl.BlockSpec(memory_space=pl.ANY)],
        out_specs=pl.BlockSpec((toks, cols), lambda i: (0, steps + i)),
        input_output_aliases={len(operands) - 1: 0},
        compiler_params=params(),
        name="place_second",
    )(*operands)


def solution(mesh):
    in_specs = (P(("dp", "seq"), None), P(), P(), P(), P(), P(), P(), P("dp"), P(("dp", "seq")))
    out_specs = P(("dp", "seq"), None)
    return jax.shard_map(
        per_device, mesh=mesh, in_specs=in_specs, out_specs=out_specs, check_vma=False
    )
```

```python
import functools
import math

import jax
import jax.numpy as jnp
from jax import lax
from jax.experimental import pallas as pl
from jax.experimental.pallas import tpu as pltpu
from jax.sharding import PartitionSpec as P

H = 32
SHORTEN = 4
KCONV = 4
PANEL = 4
BACK = 2
PAD = 8
EDGE = 16
MARK = 2.0**120
BATCH = 8
MIB = 1024 * 1024
F32 = jnp.float32
BF16 = jnp.bfloat16


def iota(shape, dim):
    return lax.broadcasted_iota(jnp.int32, shape, dim)


def project_kernel(
    lens_hbm, x_hbm, taps_hbm, gain_hbm, wk_hbm, wv_hbm, wd_hbm,
    out_ref, short_ref, lat_ref, edge_ref,
    lens_ref, x_ref, taps_ref, gain_ref, w_ref, sems, wsems, wide_ref, keep_ref, u_ref, acc_ref, fold_ref,
):
    n_bytes, byte_dim = x_ref.shape
    toks, width = short_ref.shape
    kv = wk_hbm.shape[1]
    rank = wd_hbm.shape[1]
    me = lax.axis_index("seq")
    pieces = 2
    some = n_bytes // pieces
    large = [
        pltpu.make_async_copy(
            x_hbm.at[pl.ds(i * some, some)], x_ref.at[pl.ds(i * some, some)], sems.at[3 + i]
        )
        for i in range(pieces)
    ]
    small = [
        pltpu.make_async_copy(lens_hbm, lens_ref, sems.at[0]),
        pltpu.make_async_copy(taps_hbm, taps_ref, sems.at[1]),
        pltpu.make_async_copy(gain_hbm, gain_ref, sems.at[2]),
    ]
    weights = []
    for i in range(SHORTEN):
        at = pl.ds(i * byte_dim, byte_dim)
        weights.append(
            [
                pltpu.make_async_copy(wk_hbm.at[at], w_ref.at[at, pl.ds(0, kv)], wsems.at[i, 0]),
                pltpu.make_async_copy(wv_hbm.at[at], w_ref.at[at, pl.ds(kv, kv)], wsems.at[i, 1]),
                pltpu.make_async_copy(wd_hbm.at[at], w_ref.at[at, pl.ds(2 * kv, rank)], wsems.at[i, 2]),
            ]
        )
    for copy in small + large:
        copy.start()
    for group in weights:
        for copy in group:
            copy.start(priority=1)
    for c in range(byte_dim // 128):
        wide_ref[c, 0:PAD, :] = jnp.zeros((PAD, 128), F32)
        wide_ref[c, PAD + n_bytes :, :] = jnp.zeros((PAD, 128), F32)
    u_ref[toks:, :] = jnp.zeros((EDGE, width), BF16)
    for copy in small:
        copy.wait()
    token = me * toks + iota((toks + 8, 128), 0)

    def doc(d, carry):
        first, keep = carry
        return first + lens_ref[d], jnp.where(token == first, 0.0, keep)

    _, keep = lax.fori_loop(
        0, lens_ref.shape[0], doc, (jnp.int32(0), jnp.ones((toks + 8, 128), F32))
    )
    keep_ref[...] = keep
    for i, copy in enumerate(large):
        copy.wait()
        for c in range(byte_dim // 128):
            wide_ref[c, PAD + i * some : PAD + (i + 1) * some, :] = x_ref[
                i * some : (i + 1) * some, c * 128 : (c + 1) * 128
            ].astype(F32)

    part = width // 8
    squares = [jnp.zeros((toks, 128), F32)]

    def conv(slot):
        for c in range(byte_dim // 128):
            cols = slice(c * 128, (c + 1) * 128)
            at = slot * byte_dim + c * 128
            here = jnp.zeros((toks, 128), F32)
            before = jnp.zeros((toks, 128), F32)
            corr = jnp.zeros((1, 128), F32)
            for tap in range(KCONV):
                weight = taps_ref[tap : tap + 1, cols]
                term = wide_ref[c, pl.ds(PAD + slot - tap, toks, stride=SHORTEN), :] * weight
                if tap > slot:
                    before = before + term
                    spot = PAD + n_bytes + slot - tap
                    corr = corr + wide_ref[c, spot : spot + 1, :] * weight
                else:
                    here = here + term
            if slot < KCONV - 1:
                here = here + before * keep_ref[0:toks, :]
                corr = corr * keep_ref[toks : toks + 1, :]
            short = here.astype(BF16)
            short_ref[:, at : at + 128] = short
            short = short.astype(F32)
            squares[0] = squares[0] + short * short
            gain = gain_ref[:, at : at + 128]
            u_ref[0:toks, at : at + 128] = (short * gain).astype(BF16)
            row = iota((EDGE, 128), 0)
            u_ref[toks:, at : at + 128] = jnp.where(row == 0, corr * gain, 0.0).astype(BF16)
            r, o = at // part, at % part
            fold_ref[r : r + 1, o : o + 128] = short[0:1]
            fold_ref[8 + r : 9 + r, o : o + 128] = corr

    def project(first, count):
        for group in weights[first : first + count]:
            for copy in group:
                copy.wait()
        span = slice(first * byte_dim, (first + count) * byte_dim)
        return jnp.dot(u_ref[:, span], w_ref[span, :], preferred_element_type=F32)

    middle = SHORTEN // 2
    for slot in range(middle):
        conv(slot)
    acc_ref[...] = project(0, middle)
    for slot in range(middle, SHORTEN):
        conv(slot)
    acc_ref[...] += project(middle, SHORTEN - middle)
    rs = lax.rsqrt(jnp.sum(squares[0], axis=1, keepdims=True) * (1.0 / width) + 1e-06)
    out_ref[0:toks, :] = (acc_ref[0:toks, 0 : 2 * kv] * rs).astype(BF16)
    lat_ref[...] = (acc_ref[0:toks, 2 * kv :] * rs).astype(BF16)
    edge_ref[...] = acc_ref[0:8, :]
    row = iota((EDGE, 2 * kv), 0)
    low = jnp.concatenate(
        [acc_ref[toks : toks + 1, 2 * kv :], jnp.zeros((1, 2 * kv - rank), F32)], axis=1
    )
    sums = jnp.where(row == 0, acc_ref[0:1, 0 : 2 * kv], 0.0)
    sums = jnp.where(row == 1, acc_ref[toks : toks + 1, 0 : 2 * kv], sums)
    out_ref[toks : toks + EDGE, :] = jnp.where(row == 2, low, sums).astype(BF16)
    out_ref[toks + EDGE : toks + 2 * EDGE, 0:part] = fold_ref[...].astype(BF16)


def plan_kernel(n_seq, rows, lens_ref, dest_ref, bias_ref, pick_ref):
    toks, keys = bias_ref.shape
    me = lax.axis_index("seq")
    pos = me * toks + iota((toks, 128), 0)

    def doc(d, carry):
        first, begin = carry
        return first + lens_ref[d], jnp.where(pos >= first, first, begin)

    _, begin = lax.fori_loop(
        0, lens_ref.shape[0], doc, (jnp.int32(0), jnp.zeros((toks, 128), jnp.int32))
    )
    for at in range(0, keys, 128):
        key = (me - BACK) * toks + at + iota((toks, 128), 1)
        bias_ref[:, at : at + 128] = jnp.where((key >= begin) & (key <= pos), 0.0, -1e30)
    lane = iota((8, toks), 1)
    panel = lane // PANEL
    dest = jnp.full((8, toks), -1, jnp.int32)
    for p in range(toks // PANEL):
        dest = jnp.where(panel == p, dest_ref[p], dest)
    rank = jnp.zeros((8, toks), jnp.int32)
    for p in range(toks // PANEL):
        rank = rank + jnp.where((panel > p) & (dest == dest_ref[p]), 1, 0)
    place = (dest ^ me) * rows + rank * PANEL + lane % PANEL
    row = iota((n_seq * rows, toks), 0)
    pick_ref[...] = jnp.where(row == place[0:1], 1.0, 0.0).astype(BF16)


def put_blocks(pick, layer, refs):
    empty = (1.0 - jnp.sum(pick.astype(F32), axis=1, keepdims=True)) * MARK
    placed = (jnp.dot(pick, layer, preferred_element_type=F32) + empty).astype(BF16)
    rows = refs[0].shape[0]
    for k, ref in enumerate(refs):
        ref[...] = placed[k * rows : (k + 1) * rows]


def attend_kernel(half, batch, lat_ref, edge_ref, own_ref, one_ref, two_ref, bias_ref, pick_ref, wq_ref, short_ref, *refs):
    refs, (k_ref, v_ref, query_ref, corr_ref, layer_ref) = refs[:-5], refs[-5:]
    if half == 0:
        cross_refs, out_layer_ref = refs[:-1], refs[-1]
    else:
        past_ref, refs = refs[0], refs[1:]
        cross_refs, near_refs = refs[: len(refs) // 2], refs[len(refs) // 2 :]
    toks, hd = lat_ref.shape
    wide = layer_ref.shape[1]
    heads = wide // hd
    kv = own_ref.shape[1] // 2
    part = own_ref.shape[1]
    width = 8 * part
    keys = bias_ref.shape[1]

    def root(first):
        total = jnp.sum(jnp.sum(first * first, axis=1, keepdims=True), axis=0, keepdims=True)
        return lax.rsqrt(total * (1.0 / width) + 1e-06)

    fold = slice(toks + EDGE, toks + 2 * EDGE)
    sums = slice(toks, toks + EDGE)
    own_fold = own_ref[fold, :].astype(F32)
    one_fold = one_ref[fold, :].astype(F32)
    two_fold = two_ref[fold, :].astype(F32)
    one_sums = one_ref[sums, :].astype(F32)
    two_sums = two_ref[sums, :].astype(F32)
    scale = root((own_fold[0:8] + one_fold[8:16]).astype(BF16).astype(F32))
    own_kv = scale * (edge_ref[0:1, 0 : 2 * kv] + one_sums[1:2])
    own_lat = scale * (edge_ref[0:1, 2 * kv :] + one_sums[2:3, 0:hd])
    scale = root((one_fold[0:8] + two_fold[8:16]).astype(BF16).astype(F32))
    one_kv = scale * (one_sums[0:1] + two_sums[1:2])
    row = iota((EDGE, 2 * kv), 0)
    tops = [
        two_ref[0:EDGE, :],
        jnp.where(row == 0, one_kv, one_ref[0:EDGE, :].astype(F32)).astype(BF16),
        jnp.where(row == 0, own_kv, own_ref[0:EDGE, :].astype(F32)).astype(BF16),
    ]
    k_cols = slice(half * hd, (half + 1) * hd)
    v_cols = slice(kv + half * hd, kv + (half + 1) * hd)
    for b, ref in enumerate((two_ref, one_ref, own_ref)):
        at = b * toks
        k_ref[at : at + EDGE, :] = tops[b][:, k_cols]
        k_ref[at + EDGE : at + toks, :] = ref[EDGE:toks, k_cols]
        v_ref[at : at + EDGE, 0:hd] = tops[b][:, v_cols]
        v_ref[at + EDGE : at + toks, 0:hd] = ref[EDGE:toks, v_cols]
        v_ref[at : at + toks, hd:] = jnp.ones((toks, hd), BF16)
    row = iota((EDGE, hd), 0)
    query_ref[0:EDGE, :] = jnp.where(row == 0, own_lat, lat_ref[0:EDGE, :].astype(F32)).astype(BF16)
    query_ref[EDGE:, :] = lat_ref[EDGE:, :]
    for c in range(wide // part):
        at = half * (wide // part) + c
        corr_ref[:, c * part : (c + 1) * part] = one_fold[8 + at : 9 + at]

    log_scale = math.log2(math.e) / math.sqrt(hd)
    wq = wq_ref[:, half * wide : (half + 1) * wide]
    query = (jnp.dot(query_ref[...], wq, preferred_element_type=F32) * log_scale).astype(BF16)
    key_all, value_all = k_ref[...], v_ref[...]
    for at in range(0, heads, batch):
        part_q = [query[:, h * hd : (h + 1) * hd] for h in range(at, at + batch)]
        scores = lax.dot_general(
            jnp.concatenate(part_q, axis=0), key_all, (((1,), (1,)), ((), ())), preferred_element_type=F32
        )
        scores = scores.reshape(batch, toks, keys) + bias_ref[...][None]
        top = jnp.max(scores, axis=2, keepdims=True)
        probs = jnp.exp2(scores - top).astype(BF16).reshape(batch * toks, keys)
        mixed = jnp.dot(probs, value_all, preferred_element_type=F32)
        mixed = mixed[:, 0:hd] / mixed[:, hd:]
        for h in range(batch):
            cols = slice((at + h) * hd, (at + h + 1) * hd)
            short = short_ref[:, half * wide + (at + h) * hd : half * wide + (at + h + 1) * hd].astype(F32)
            whole = (short[0:8] + corr_ref[:, cols]).astype(BF16).astype(F32)
            first = jnp.where(iota((8, hd), 0) == 0, whole, short[0:8])
            short = jnp.concatenate([first, short[8:]], axis=0)
            layer_ref[:, cols] = (mixed[h * toks : (h + 1) * toks] + short).astype(BF16)
    middle = pick_ref.shape[0] // 2
    put_blocks(pick_ref[middle:, :], layer_ref[...], cross_refs)
    if half == 0:
        out_layer_ref[...] = layer_ref[...]
    else:
        layer = jnp.concatenate([past_ref[...], layer_ref[...]], axis=1)
        put_blocks(pick_ref[0:middle, :], layer, near_refs)


def first_kernel(n_seq, rows, *refs):
    block_refs, (out_ref, sel_ref, pick_ref) = refs[:-3], refs[-3:]
    toks = out_ref.shape[0]
    got = jnp.concatenate([r[...] for r in block_refs], axis=0)
    me = lax.axis_index("seq")

    @pl.when(pl.program_id(0) == 0)
    def _():
        n_pad = max(16, n_seq)
        n_rows = got.shape[0]
        used = jnp.where(got[:, 0:128].astype(F32) < 0.5 * MARK, 1.0, 0.0).astype(BF16)
        member = iota((n_pad, n_rows), 0) == iota((n_pad, n_rows), 1) // rows
        count = jnp.dot(jnp.where(member, 1.0, 0.0).astype(BF16), used, preferred_element_type=F32)
        source = me ^ iota((n_pad, 128), 0)
        offset = jnp.zeros((n_pad, 128), F32)
        for q in range(n_seq):
            offset = offset + jnp.where(source > (me ^ q), count[q : q + 1], 0.0)
        lane = iota((1, n_rows), 1)
        within = (lane % rows).astype(F32)
        target = jnp.full((1, n_rows), -1.0, F32)
        for q in range(n_seq):
            valid = (lane // rows == q) & (within < count[q : q + 1, 0:1])
            target = jnp.where(valid, offset[q : q + 1, 0:1] + within, target)
        row = iota((toks, n_rows), 0).astype(F32)
        pick_ref[...] = jnp.where(row == target, 1.0, 0.0).astype(BF16)
        sel_ref[...] = pick_ref[...]

    out_ref[...] = jnp.dot(pick_ref[...], got, preferred_element_type=F32).astype(BF16)


def second_kernel(span, sel_ref, *refs):
    block_refs, (out_ref, stage_ref, sems) = refs[:-4], refs[-3:]
    pieces, _, cols = stage_ref.shape
    copies = []
    for i in range(pieces):
        parts = []
        for ref in block_refs:
            at = ref.shape[1] - span + i * cols
            parts.append(ref[:, at : at + cols])
        got = jnp.concatenate(parts, axis=0)
        stage_ref[i] = jnp.dot(sel_ref[...], got, preferred_element_type=F32).astype(BF16)
        copies.append(
            pltpu.make_async_copy(
                stage_ref.at[i], out_ref.at[:, pl.ds(out_ref.shape[1] - span + i * cols, cols)], sems.at[i]
            )
        )
        copies[-1].start()
    for copy in copies:
        copy.wait()


def swap(array, by, size):
    return lax.ppermute(array, "seq", [(i, i ^ by) for i in range(size)])


def smem():
    return pl.BlockSpec(memory_space=pltpu.SMEM)


def vmem():
    return pl.BlockSpec(memory_space=pltpu.VMEM)


def hbm():
    return pl.BlockSpec(memory_space=pltpu.HBM)


def in_hbm(array):
    return pltpu.with_memory_space_constraint(array, pltpu.HBM)


def whole_block(shape):
    return pl.BlockSpec(shape, lambda i: (0,) * len(shape))


def column_block(rows, cols):
    return pl.BlockSpec((rows, cols), lambda i: (0, i))


def params(limit=32 * MIB):
    return pltpu.CompilerParams(vmem_limit_bytes=limit)


def per_device(
    byte_embed, conv_taps, norm_gain, w_qdown, w_qup, w_key, w_value, doc_lengths, panel_dest
):
    n_seq = lax.axis_size("seq")
    n_bytes, byte_dim = byte_embed.shape
    toks = n_bytes // SHORTEN
    width = SHORTEN * byte_dim
    hd = width // H
    kv = w_key.shape[1]
    kvh = kv // hd
    rank = w_qdown.shape[1]
    pans = toks // PANEL
    slots = (2 * pans + n_seq - 1) // n_seq
    rows = slots * PANEL
    merged = rows % 16 != 0
    keys = (BACK + 1) * toks
    held_rows = toks + 2 * EDGE

    held, short, latent, edge = pl.pallas_call(
        project_kernel,
        out_shape=[
            pltpu.VMEM((held_rows, 2 * kv), BF16),
            pltpu.VMEM((toks, width), BF16),
            pltpu.VMEM((toks, rank), BF16),
            pltpu.VMEM((8, 2 * kv + rank), F32),
        ],
        in_specs=[hbm()] * 7,
        out_specs=[vmem()] * 4,
        scratch_shapes=[
            pltpu.SMEM(doc_lengths.shape, jnp.int32),
            pltpu.VMEM((n_bytes, byte_dim), BF16),
            pltpu.VMEM((KCONV, byte_dim), F32),
            pltpu.VMEM((1, width), F32),
            pltpu.VMEM((width, 2 * kv + rank), BF16),
            pltpu.SemaphoreType.DMA((5,)),
            pltpu.SemaphoreType.DMA((SHORTEN, 3)),
            pltpu.VMEM((byte_dim // 128, n_bytes + 2 * PAD, 128), F32),
            pltpu.VMEM((toks + 8, 128), F32),
            pltpu.VMEM((toks + EDGE, width), BF16),
            pltpu.VMEM((toks + EDGE, 2 * kv + rank), F32),
            pltpu.VMEM((16, width // 8), F32),
        ],
        compiler_params=params(24 * MIB),
        name="project",
    )(
        *[
            in_hbm(a)
            for a in (
                doc_lengths, byte_embed, conv_taps, norm_gain.reshape(1, width), w_key, w_value, w_qdown
            )
        ]
    )

    behind = [
        lax.ppermute(held, "seq", [(i, i + by) for i in range(n_seq - by)])
        for by in range(1, BACK + 1)
    ]

    bias, pick = pl.pallas_call(
        functools.partial(plan_kernel, n_seq, rows),
        out_shape=[
            pltpu.VMEM((toks, keys), F32),
            pltpu.VMEM((n_seq * rows, toks), BF16),
        ],
        in_specs=[smem()] * 2,
        out_specs=[vmem()] * 2,
        compiler_params=params(),
        name="plan",
    )(doc_lengths, panel_dest)

    middle = n_seq // 2
    span = width // kvh
    batch = BATCH
    n_out, out_rows = (1, middle * rows) if merged else (middle, rows)

    def split(blocks):
        if merged:
            return [blocks[0][k * rows : (k + 1) * rows] for k in range(middle)]
        return list(blocks)

    def attend(half, more):
        cross = [pltpu.VMEM((out_rows, span), BF16)] * n_out
        near = [pltpu.VMEM((out_rows, width), BF16)] * n_out
        outs = cross + ([pltpu.VMEM((toks, span), BF16)] if half == 0 else near)
        operands = [latent, edge, held, *behind, bias, pick, w_qup, short, *more]
        return pl.pallas_call(
            functools.partial(attend_kernel, half, batch),
            out_shape=outs,
            in_specs=[vmem()] * len(operands),
            out_specs=[vmem()] * len(outs),
            scratch_shapes=[
                pltpu.VMEM((keys, hd), BF16),
                pltpu.VMEM((keys, 2 * hd), BF16),
                pltpu.VMEM((toks, rank), BF16),
                pltpu.VMEM((1, span), F32),
                pltpu.VMEM((toks, span), BF16),
            ],
            compiler_params=params(),
            name=f"attend_half_{half}",
        )(*operands)

    *first_cross, layer = attend(0, [])
    got_first = [swap(x, middle + k, n_seq) for k, x in enumerate(split(first_cross))]
    outs = attend(1, [layer])
    got_second = [swap(x, middle + k, n_seq) for k, x in enumerate(split(outs[:n_out]))]
    near = split(outs[n_out:])
    got_near = [near[0]] + [swap(near[k], k, n_seq) for k in range(1, middle)]
    if merged:
        got_first, got_second, got_near = (
            [jnp.concatenate(g, axis=0)] for g in (got_first, got_second, got_near)
        )

    steps = 4
    cols = span // steps

    def columns(arrays, start):
        return [pl.BlockSpec((a.shape[0], cols), lambda i: (0, start + i)) for a in arrays]

    out, sel = pl.pallas_call(
        functools.partial(first_kernel, n_seq, rows),
        grid=(steps,),
        out_shape=[
            jax.ShapeDtypeStruct((toks, width), BF16),
            jax.ShapeDtypeStruct((toks, n_seq * rows), BF16),
        ],
        in_specs=columns(got_near, 0) + columns(got_first, 0),
        out_specs=[
            pl.BlockSpec((toks, cols), lambda i: (0, i)),
            whole_block((toks, n_seq * rows)),
        ],
        scratch_shapes=[pltpu.VMEM((toks, n_seq * rows), BF16)],
        compiler_params=params(),
        name="place_first",
    )(*got_near, *got_first)
    operands = [sel, *got_near, *got_second, out]
    return pl.pallas_call(
        functools.partial(second_kernel, span),
        out_shape=jax.ShapeDtypeStruct((toks, width), BF16),
        in_specs=[vmem()] * (len(operands) - 1) + [pl.BlockSpec(memory_space=pl.ANY)],
        out_specs=pl.BlockSpec(memory_space=pl.ANY),
        scratch_shapes=[pltpu.VMEM((steps, toks, cols), BF16), pltpu.SemaphoreType.DMA((steps,))],
        input_output_aliases={len(operands) - 1: 0},
        compiler_params=params(),
        name="place_second",
    )(*operands)


def solution(mesh):
    in_specs = (P(("dp", "seq"), None), P(), P(), P(), P(), P(), P(), P("dp"), P(("dp", "seq")))
    out_specs = P(("dp", "seq"), None)
    return jax.shard_map(
        per_device, mesh=mesh, in_specs=in_specs, out_specs=out_specs, check_vma=False
    )
```

```python
import functools
import math

import jax
import jax.numpy as jnp
from jax import lax
from jax.experimental import pallas as pl
from jax.experimental.pallas import tpu as pltpu
from jax.sharding import PartitionSpec as P

H = 32
SHORTEN = 4
KCONV = 4
PANEL = 4
BACK = 2
PAD = 8
EDGE = 16
MARK = 2.0**120
BATCH = 8
MIB = 1024 * 1024
F32 = jnp.float32
BF16 = jnp.bfloat16


def iota(shape, dim):
    return lax.broadcasted_iota(jnp.int32, shape, dim)


def project_kernel(
    lens_hbm, x_hbm, taps_hbm, gain_hbm, wk_hbm, wv_hbm, wd_hbm,
    out_ref, short_ref, lat_ref, edge_ref,
    lens_ref, x_ref, taps_ref, gain_ref, w_ref, sems, wsems, wide_ref, keep_ref, u_ref, acc_ref, fold_ref,
):
    n_bytes, byte_dim = x_ref.shape
    toks, width = short_ref.shape
    kv = wk_hbm.shape[1]
    rank = wd_hbm.shape[1]
    me = lax.axis_index("seq")
    pieces = 2
    some = n_bytes // pieces
    large = [
        pltpu.make_async_copy(
            x_hbm.at[pl.ds(i * some, some)], x_ref.at[pl.ds(i * some, some)], sems.at[3 + i]
        )
        for i in range(pieces)
    ]
    small = [
        pltpu.make_async_copy(lens_hbm, lens_ref, sems.at[0]),
        pltpu.make_async_copy(taps_hbm, taps_ref, sems.at[1]),
        pltpu.make_async_copy(gain_hbm, gain_ref, sems.at[2]),
    ]
    weights = []
    for i in range(SHORTEN):
        at = pl.ds(i * byte_dim, byte_dim)
        weights.append(
            [
                pltpu.make_async_copy(wk_hbm.at[at], w_ref.at[at, pl.ds(0, kv)], wsems.at[i, 0]),
                pltpu.make_async_copy(wv_hbm.at[at], w_ref.at[at, pl.ds(kv, kv)], wsems.at[i, 1]),
                pltpu.make_async_copy(wd_hbm.at[at], w_ref.at[at, pl.ds(2 * kv, rank)], wsems.at[i, 2]),
            ]
        )
    for copy in small + large:
        copy.start()
    for group in weights:
        for copy in group:
            copy.start(priority=1)
    for c in range(byte_dim // 128):
        wide_ref[c, 0:PAD, :] = jnp.zeros((PAD, 128), F32)
        wide_ref[c, PAD + n_bytes :, :] = jnp.zeros((PAD, 128), F32)
    u_ref[toks:, :] = jnp.zeros((EDGE, width), BF16)
    for copy in small:
        copy.wait()
    token = me * toks + iota((toks + 8, 128), 0)

    def doc(d, carry):
        first, keep = carry
        return first + lens_ref[d], jnp.where(token == first, 0.0, keep)

    _, keep = lax.fori_loop(
        0, lens_ref.shape[0], doc, (jnp.int32(0), jnp.ones((toks + 8, 128), F32))
    )
    keep_ref[...] = keep
    for i, copy in enumerate(large):
        copy.wait()
        for c in range(byte_dim // 128):
            wide_ref[c, PAD + i * some : PAD + (i + 1) * some, :] = x_ref[
                i * some : (i + 1) * some, c * 128 : (c + 1) * 128
            ].astype(F32)

    part = width // 8
    squares = [jnp.zeros((toks, 128), F32)]

    def conv(slot):
        for c in range(byte_dim // 128):
            cols = slice(c * 128, (c + 1) * 128)
            at = slot * byte_dim + c * 128
            here = jnp.zeros((toks, 128), F32)
            before = jnp.zeros((toks, 128), F32)
            corr = jnp.zeros((1, 128), F32)
            for tap in range(KCONV):
                weight = taps_ref[tap : tap + 1, cols]
                term = wide_ref[c, pl.ds(PAD + slot - tap, toks, stride=SHORTEN), :] * weight
                if tap > slot:
                    before = before + term
                    spot = PAD + n_bytes + slot - tap
                    corr = corr + wide_ref[c, spot : spot + 1, :] * weight
                else:
                    here = here + term
            if slot < KCONV - 1:
                here = here + before * keep_ref[0:toks, :]
                corr = corr * keep_ref[toks : toks + 1, :]
            short = here.astype(BF16)
            short_ref[:, at : at + 128] = short
            short = short.astype(F32)
            squares[0] = squares[0] + short * short
            gain = gain_ref[:, at : at + 128]
            u_ref[0:toks, at : at + 128] = (short * gain).astype(BF16)
            row = iota((EDGE, 128), 0)
            u_ref[toks:, at : at + 128] = jnp.where(row == 0, corr * gain, 0.0).astype(BF16)
            r, o = at // part, at % part
            fold_ref[r : r + 1, o : o + 128] = short[0:1]
            fold_ref[8 + r : 9 + r, o : o + 128] = corr

    def project(first, count):
        for group in weights[first : first + count]:
            for copy in group:
                copy.wait()
        span = slice(first * byte_dim, (first + count) * byte_dim)
        return jnp.dot(u_ref[:, span], w_ref[span, :], preferred_element_type=F32)

    middle = SHORTEN // 2
    for slot in range(middle):
        conv(slot)
    acc_ref[...] = project(0, middle)
    for slot in range(middle, SHORTEN):
        conv(slot)
    acc_ref[...] += project(middle, SHORTEN - middle)
    rs = lax.rsqrt(jnp.sum(squares[0], axis=1, keepdims=True) * (1.0 / width) + 1e-06)
    out_ref[0:toks, :] = (acc_ref[0:toks, 0 : 2 * kv] * rs).astype(BF16)
    lat_ref[...] = (acc_ref[0:toks, 2 * kv :] * rs).astype(BF16)
    edge_ref[...] = acc_ref[0:8, :]
    row = iota((EDGE, 2 * kv), 0)
    low = jnp.concatenate(
        [acc_ref[toks : toks + 1, 2 * kv :], jnp.zeros((1, 2 * kv - rank), F32)], axis=1
    )
    sums = jnp.where(row == 0, acc_ref[0:1, 0 : 2 * kv], 0.0)
    sums = jnp.where(row == 1, acc_ref[toks : toks + 1, 0 : 2 * kv], sums)
    out_ref[toks : toks + EDGE, :] = jnp.where(row == 2, low, sums).astype(BF16)
    out_ref[toks + EDGE : toks + 2 * EDGE, 0:part] = fold_ref[...].astype(BF16)


def plan_kernel(n_seq, rows, lens_ref, dest_ref, bias_ref, pick_ref):
    toks, keys = bias_ref.shape
    me = lax.axis_index("seq")
    pos = me * toks + iota((toks, 128), 0)

    def doc(d, carry):
        first, begin = carry
        return first + lens_ref[d], jnp.where(pos >= first, first, begin)

    _, begin = lax.fori_loop(
        0, lens_ref.shape[0], doc, (jnp.int32(0), jnp.zeros((toks, 128), jnp.int32))
    )
    for at in range(0, keys, 128):
        key = (me - BACK) * toks + at + iota((toks, 128), 1)
        bias_ref[:, at : at + 128] = jnp.where((key >= begin) & (key <= pos), 0.0, -1e30)
    lane = iota((8, toks), 1)
    panel = lane // PANEL
    dest = jnp.full((8, toks), -1, jnp.int32)
    for p in range(toks // PANEL):
        dest = jnp.where(panel == p, dest_ref[p], dest)
    rank = jnp.zeros((8, toks), jnp.int32)
    for p in range(toks // PANEL):
        rank = rank + jnp.where((panel > p) & (dest == dest_ref[p]), 1, 0)
    place = (dest ^ me) * rows + rank * PANEL + lane % PANEL
    row = iota((n_seq * rows, toks), 0)
    pick_ref[...] = jnp.where(row == place[0:1], 1.0, 0.0).astype(BF16)


def put_blocks(pick, layer, refs):
    empty = (1.0 - jnp.sum(pick.astype(F32), axis=1, keepdims=True)) * MARK
    placed = (jnp.dot(pick, layer, preferred_element_type=F32) + empty).astype(BF16)
    rows = refs[0].shape[0]
    for k, ref in enumerate(refs):
        ref[...] = placed[k * rows : (k + 1) * rows]


def attend_kernel(half, batch, n_cross, lat_ref, edge_ref, own_ref, one_ref, two_ref, bias_ref, pick_ref, wq_ref, short_ref, *refs):
    refs, (k_ref, v_ref, query_ref, corr_ref, layer_ref) = refs[:-5], refs[-5:]
    if half == 0:
        cross_refs, out_layer_ref = refs[:-1], refs[-1]
    else:
        past_ref, refs = refs[0], refs[1:]
        cross_refs, far_refs, near_refs = refs[:n_cross], refs[n_cross : 2 * n_cross], refs[2 * n_cross :]
    toks, hd = lat_ref.shape
    wide = layer_ref.shape[1]
    heads = wide // hd
    kv = own_ref.shape[1] // 2
    part = own_ref.shape[1]
    width = 8 * part
    keys = bias_ref.shape[1]

    def root(first):
        total = jnp.sum(jnp.sum(first * first, axis=1, keepdims=True), axis=0, keepdims=True)
        return lax.rsqrt(total * (1.0 / width) + 1e-06)

    fold = slice(toks + EDGE, toks + 2 * EDGE)
    sums = slice(toks, toks + EDGE)
    own_fold = own_ref[fold, :].astype(F32)
    one_fold = one_ref[fold, :].astype(F32)
    two_fold = two_ref[fold, :].astype(F32)
    one_sums = one_ref[sums, :].astype(F32)
    two_sums = two_ref[sums, :].astype(F32)
    scale = root((own_fold[0:8] + one_fold[8:16]).astype(BF16).astype(F32))
    own_kv = scale * (edge_ref[0:1, 0 : 2 * kv] + one_sums[1:2])
    own_lat = scale * (edge_ref[0:1, 2 * kv :] + one_sums[2:3, 0:hd])
    scale = root((one_fold[0:8] + two_fold[8:16]).astype(BF16).astype(F32))
    one_kv = scale * (one_sums[0:1] + two_sums[1:2])
    row = iota((EDGE, 2 * kv), 0)
    tops = [
        two_ref[0:EDGE, :],
        jnp.where(row == 0, one_kv, one_ref[0:EDGE, :].astype(F32)).astype(BF16),
        jnp.where(row == 0, own_kv, own_ref[0:EDGE, :].astype(F32)).astype(BF16),
    ]
    k_cols = slice(half * hd, (half + 1) * hd)
    v_cols = slice(kv + half * hd, kv + (half + 1) * hd)
    for b, ref in enumerate((two_ref, one_ref, own_ref)):
        at = b * toks
        k_ref[at : at + EDGE, :] = tops[b][:, k_cols]
        k_ref[at + EDGE : at + toks, :] = ref[EDGE:toks, k_cols]
        v_ref[at : at + EDGE, 0:hd] = tops[b][:, v_cols]
        v_ref[at + EDGE : at + toks, 0:hd] = ref[EDGE:toks, v_cols]
        v_ref[at : at + toks, hd:] = jnp.ones((toks, hd), BF16)
    row = iota((EDGE, hd), 0)
    query_ref[0:EDGE, :] = jnp.where(row == 0, own_lat, lat_ref[0:EDGE, :].astype(F32)).astype(BF16)
    query_ref[EDGE:, :] = lat_ref[EDGE:, :]
    for c in range(wide // part):
        at = half * (wide // part) + c
        corr_ref[:, c * part : (c + 1) * part] = one_fold[8 + at : 9 + at]

    log_scale = math.log2(math.e) / math.sqrt(hd)
    wq = wq_ref[:, half * wide : (half + 1) * wide]
    query = (jnp.dot(query_ref[...], wq, preferred_element_type=F32) * log_scale).astype(BF16)
    key_all, value_all = k_ref[...], v_ref[...]
    for at in range(0, heads, batch):
        part_q = [query[:, h * hd : (h + 1) * hd] for h in range(at, at + batch)]
        scores = lax.dot_general(
            jnp.concatenate(part_q, axis=0), key_all, (((1,), (1,)), ((), ())), preferred_element_type=F32
        )
        scores = scores.reshape(batch, toks, keys) + bias_ref[...][None]
        top = jnp.max(scores, axis=2, keepdims=True)
        probs = jnp.exp2(scores - top).astype(BF16).reshape(batch * toks, keys)
        mixed = jnp.dot(probs, value_all, preferred_element_type=F32)
        mixed = mixed[:, 0:hd] / mixed[:, hd:]
        for h in range(batch):
            cols = slice((at + h) * hd, (at + h + 1) * hd)
            short = short_ref[:, half * wide + (at + h) * hd : half * wide + (at + h + 1) * hd].astype(F32)
            whole = (short[0:8] + corr_ref[:, cols]).astype(BF16).astype(F32)
            first = jnp.where(iota((8, hd), 0) == 0, whole, short[0:8])
            short = jnp.concatenate([first, short[8:]], axis=0)
            layer_ref[:, cols] = (mixed[h * toks : (h + 1) * toks] + short).astype(BF16)
    middle = pick_ref.shape[0] // 2
    far = middle + middle // 2
    put_blocks(pick_ref[middle:far, :], layer_ref[...], cross_refs)
    if half == 0:
        out_layer_ref[...] = layer_ref[...]
    else:
        layer = jnp.concatenate([past_ref[...], layer_ref[...]], axis=1)
        put_blocks(pick_ref[far:, :], layer, far_refs)
        put_blocks(pick_ref[0:middle, :], layer, near_refs)


def read_parts(parts, refs, at, cols):
    return jnp.concatenate([refs[i][row : row + rows, col + at : col + at + cols] for i, row, rows, col in parts], axis=0)


def count_marks(first, block, rows, n_pad):
    used = jnp.where(rows.astype(F32) < 0.5 * MARK, 1.0, 0.0).astype(BF16)
    shape = (n_pad, rows.shape[0])
    member = iota(shape, 0) == first + iota(shape, 1) // block
    return jnp.dot(jnp.where(member, 1.0, 0.0).astype(BF16), used, preferred_element_type=F32)


def count_kernel(first, block, parts, *refs):
    count_ref = refs[-1]
    count_ref[...] = count_marks(first, block, read_parts(parts, refs, 0, 128), count_ref.shape[0])


def place_kernel(n_seq, block, near, half, parts, *refs):
    if half == 0:
        count_ref, *got_refs, out_ref, sel_ref, stage_ref, sems = refs
    else:
        sel_ref, *got_refs, _, out_ref, stage_ref, sems = refs
    pieces, toks, cols = stage_ref.shape
    if half == 0:
        me = lax.axis_index("seq")
        n_pad = count_ref.shape[0]
        n_rows = n_seq * block
        head = read_parts(parts, got_refs, 0, 128)[near * block :]
        count = count_ref[...] + count_marks(near, block, head, n_pad)
        source = me ^ iota((n_pad, 128), 0)
        offset = jnp.zeros((n_pad, 128), F32)
        for q in range(n_seq):
            offset = offset + jnp.where(source > (me ^ q), count[q : q + 1], 0.0)
        lane = iota((1, n_rows), 1)
        within = (lane % block).astype(F32)
        target = jnp.full((1, n_rows), -1.0, F32)
        for q in range(n_seq):
            valid = (lane // block == q) & (within < count[q : q + 1, 0:1])
            target = jnp.where(valid, offset[q : q + 1, 0:1] + within, target)
        sel_ref[...] = jnp.where(iota((toks, n_rows), 0).astype(F32) == target, 1.0, 0.0).astype(BF16)
    copies = []
    for i in range(pieces):
        got = read_parts(parts, got_refs, i * cols, cols)
        stage_ref[i] = jnp.dot(sel_ref[...], got, preferred_element_type=F32).astype(BF16)
        at = half * pieces * cols + i * cols
        copies.append(
            pltpu.make_async_copy(stage_ref.at[i], out_ref.at[:, pl.ds(at, cols)], sems.at[i])
        )
        copies[-1].start()
    for copy in copies:
        copy.wait()


def swap(array, by, size):
    return lax.ppermute(array, "seq", [(i, i ^ by) for i in range(size)])


def smem():
    return pl.BlockSpec(memory_space=pltpu.SMEM)


def vmem():
    return pl.BlockSpec(memory_space=pltpu.VMEM)


def hbm():
    return pl.BlockSpec(memory_space=pltpu.HBM)


def in_hbm(array):
    return pltpu.with_memory_space_constraint(array, pltpu.HBM)


def whole_block(shape):
    return pl.BlockSpec(shape, lambda i: (0,) * len(shape))


def column_block(rows, cols):
    return pl.BlockSpec((rows, cols), lambda i: (0, i))


def params(limit=32 * MIB):
    return pltpu.CompilerParams(vmem_limit_bytes=limit)


def per_device(
    byte_embed, conv_taps, norm_gain, w_qdown, w_qup, w_key, w_value, doc_lengths, panel_dest
):
    n_seq = lax.axis_size("seq")
    n_bytes, byte_dim = byte_embed.shape
    toks = n_bytes // SHORTEN
    width = SHORTEN * byte_dim
    hd = width // H
    kv = w_key.shape[1]
    kvh = kv // hd
    rank = w_qdown.shape[1]
    pans = toks // PANEL
    slots = (2 * pans + n_seq - 1) // n_seq
    rows = slots * PANEL
    merged = rows % 16 != 0
    keys = (BACK + 1) * toks
    held_rows = toks + 2 * EDGE

    held, short, latent, edge = pl.pallas_call(
        project_kernel,
        out_shape=[
            pltpu.VMEM((held_rows, 2 * kv), BF16),
            pltpu.VMEM((toks, width), BF16),
            pltpu.VMEM((toks, rank), BF16),
            pltpu.VMEM((8, 2 * kv + rank), F32),
        ],
        in_specs=[hbm()] * 7,
        out_specs=[vmem()] * 4,
        scratch_shapes=[
            pltpu.SMEM(doc_lengths.shape, jnp.int32),
            pltpu.VMEM((n_bytes, byte_dim), BF16),
            pltpu.VMEM((KCONV, byte_dim), F32),
            pltpu.VMEM((1, width), F32),
            pltpu.VMEM((width, 2 * kv + rank), BF16),
            pltpu.SemaphoreType.DMA((5,)),
            pltpu.SemaphoreType.DMA((SHORTEN, 3)),
            pltpu.VMEM((byte_dim // 128, n_bytes + 2 * PAD, 128), F32),
            pltpu.VMEM((toks + 8, 128), F32),
            pltpu.VMEM((toks + EDGE, width), BF16),
            pltpu.VMEM((toks + EDGE, 2 * kv + rank), F32),
            pltpu.VMEM((16, width // 8), F32),
        ],
        compiler_params=params(24 * MIB),
        name="project",
    )(
        *[
            in_hbm(a)
            for a in (
                doc_lengths, byte_embed, conv_taps, norm_gain.reshape(1, width), w_key, w_value, w_qdown
            )
        ]
    )

    behind = [
        lax.ppermute(held, "seq", [(i, i + by) for i in range(n_seq - by)])
        for by in range(1, BACK + 1)
    ]

    bias, pick = pl.pallas_call(
        functools.partial(plan_kernel, n_seq, rows),
        out_shape=[
            pltpu.VMEM((toks, keys), F32),
            pltpu.VMEM((n_seq * rows, toks), BF16),
        ],
        in_specs=[smem()] * 2,
        out_specs=[vmem()] * 2,
        compiler_params=params(),
        name="plan",
    )(doc_lengths, panel_dest)

    middle = n_seq // 2
    span = width // kvh
    def shapes(count, height, cols):
        count, height = (1, count * height) if merged else (count, height)
        return [pltpu.VMEM((height, cols), BF16)] * count

    def split(arrays, count):
        if len(arrays) == count:
            return list(arrays)
        height = arrays[0].shape[0] // count
        return [arrays[0][i * height : (i + 1) * height] for i in range(count)]

    def attend(half, outs, n_cross, more):
        operands = [latent, edge, held, *behind, bias, pick, w_qup, short, *more]
        return pl.pallas_call(
            functools.partial(attend_kernel, half, BATCH, n_cross),
            out_shape=outs,
            in_specs=[vmem()] * len(operands),
            out_specs=[vmem()] * len(outs),
            scratch_shapes=[
                pltpu.VMEM((keys, hd), BF16),
                pltpu.VMEM((keys, 2 * hd), BF16),
                pltpu.VMEM((toks, rank), BF16),
                pltpu.VMEM((1, span), F32),
                pltpu.VMEM((toks, span), BF16),
            ],
            compiler_params=params(),
            name=f"attend_half_{half}",
        )(*operands)

    half_cross = middle // 2
    cross = shapes(half_cross, rows, span)
    *first, layer = attend(0, cross + [pltpu.VMEM((toks, span), BF16)], len(cross), [])
    first = split(first, half_cross)
    got_first = [swap(first[k], middle + k, n_seq) for k in range(half_cross)]
    far, near = shapes(half_cross, rows, width), shapes(middle, rows, width)
    outs = attend(1, cross + far + near, len(cross), [layer])
    second, outs = split(outs[: len(cross)], half_cross), outs[len(cross) :]
    far, near = split(outs[: len(far)], half_cross), split(outs[len(far) :], middle)
    got_far = [swap(far[k], middle + half_cross + k, n_seq) for k in range(half_cross)]
    got_near = [near[0]] + [swap(near[k], k, n_seq) for k in range(1, middle)]
    got_second = [swap(second[k], middle + k, n_seq) for k in range(half_cross)]

    def parts(found):
        if merged:
            pieces = [a[r : r + rows, c : c + span] for a, r, c in found]
            return [jnp.concatenate(pieces, axis=0)], [(0, 0, len(found) * rows, 0)]
        return [a for a, _, _ in found], [(i, r, rows, c) for i, (_, r, c) in enumerate(found)]

    near_parts = [[(a, 0, half * span) for a in got_near] for half in range(kvh)]
    cross_parts = [
        [(a, 0, 0) for a in got] + [(a, 0, half * span) for a in got_far]
        for half, got in enumerate((got_first, got_second))
    ]
    arrays, where = parts(near_parts[0])
    waits = got_first
    count = pl.pallas_call(
        functools.partial(count_kernel, 0, rows, where),
        out_shape=pltpu.VMEM((max(16, n_seq), 128), F32),
        in_specs=[vmem()] * len(arrays) + [pl.BlockSpec(memory_space=pl.ANY)] * len(waits),
        out_specs=vmem(),
        compiler_params=params(),
        name="count",
    )(*arrays, *waits)

    steps = 4
    cols = span // steps
    scratch = [pltpu.VMEM((steps, toks, cols), BF16), pltpu.SemaphoreType.DMA((steps,))]
    out_shape = jax.ShapeDtypeStruct((toks, width), BF16)
    anywhere = pl.BlockSpec(memory_space=pl.ANY)
    arrays, where = parts(near_parts[0] + cross_parts[0])
    out, sel = pl.pallas_call(
        functools.partial(place_kernel, n_seq, rows, middle, 0, where),
        out_shape=[out_shape, pltpu.VMEM((toks, n_seq * rows), BF16)],
        in_specs=[vmem()] * (1 + len(arrays)),
        out_specs=[anywhere, vmem()],
        scratch_shapes=scratch,
        compiler_params=params(),
        name="place_first",
    )(count, *arrays)
    arrays, where = parts(near_parts[1] + cross_parts[1])
    return pl.pallas_call(
        functools.partial(place_kernel, n_seq, rows, middle, 1, where),
        out_shape=out_shape,
        in_specs=[vmem()] * (1 + len(arrays)) + [anywhere],
        out_specs=anywhere,
        scratch_shapes=scratch,
        input_output_aliases={1 + len(arrays): 0},
        compiler_params=params(),
        name="place_second",
    )(sel, *arrays, out)


def solution(mesh):
    in_specs = (P(("dp", "seq"), None), P(), P(), P(), P(), P(), P(), P("dp"), P(("dp", "seq")))
    out_specs = P(("dp", "seq"), None)
    return jax.shard_map(
        per_device, mesh=mesh, in_specs=in_specs, out_specs=out_specs, check_vma=False
    )
```

```python
import functools
import math

import jax
import jax.numpy as jnp
from jax import lax
from jax.experimental import pallas as pl
from jax.experimental.pallas import tpu as pltpu
from jax.sharding import PartitionSpec as P

H = 32
SHORTEN = 4
KCONV = 4
PANEL = 4
BACK = 2
PAD = 8
EDGE = 16
MARK = 2.0**120
BATCH = (8, 4)
MIB = 1024 * 1024
F32 = jnp.float32
BF16 = jnp.bfloat16


def iota(shape, dim):
    return lax.broadcasted_iota(jnp.int32, shape, dim)


def project_kernel(
    lens_hbm, x_hbm, taps_hbm, gain_hbm, wk_hbm, wv_hbm, wd_hbm,
    out_ref, short_ref, lat_ref, edge_ref,
    lens_ref, x_ref, taps_ref, gain_ref, w_ref, sems, wsems, wide_ref, keep_ref, u_ref, acc_ref, fold_ref,
):
    n_bytes, byte_dim = x_ref.shape
    toks, width = short_ref.shape
    kv = wk_hbm.shape[1]
    rank = wd_hbm.shape[1]
    me = lax.axis_index("seq")
    pieces = 2
    some = n_bytes // pieces
    large = [
        pltpu.make_async_copy(
            x_hbm.at[pl.ds(i * some, some)], x_ref.at[pl.ds(i * some, some)], sems.at[3 + i]
        )
        for i in range(pieces)
    ]
    small = [
        pltpu.make_async_copy(lens_hbm, lens_ref, sems.at[0]),
        pltpu.make_async_copy(taps_hbm, taps_ref, sems.at[1]),
        pltpu.make_async_copy(gain_hbm, gain_ref, sems.at[2]),
    ]
    weights = []
    for i in range(SHORTEN):
        at = pl.ds(i * byte_dim, byte_dim)
        weights.append(
            [
                pltpu.make_async_copy(wk_hbm.at[at], w_ref.at[at, pl.ds(0, kv)], wsems.at[i, 0]),
                pltpu.make_async_copy(wv_hbm.at[at], w_ref.at[at, pl.ds(kv, kv)], wsems.at[i, 1]),
                pltpu.make_async_copy(wd_hbm.at[at], w_ref.at[at, pl.ds(2 * kv, rank)], wsems.at[i, 2]),
            ]
        )
    for copy in small + large:
        copy.start()
    for group in weights:
        for copy in group:
            copy.start(priority=1)
    for c in range(byte_dim // 128):
        wide_ref[c, 0:PAD, :] = jnp.zeros((PAD, 128), F32)
        wide_ref[c, PAD + n_bytes :, :] = jnp.zeros((PAD, 128), F32)
    u_ref[toks:, :] = jnp.zeros((EDGE, width), BF16)
    for copy in small:
        copy.wait()
    token = me * toks + iota((toks + 8, 128), 0)

    def doc(d, carry):
        first, keep = carry
        return first + lens_ref[d], jnp.where(token == first, 0.0, keep)

    _, keep = lax.fori_loop(
        0, lens_ref.shape[0], doc, (jnp.int32(0), jnp.ones((toks + 8, 128), F32))
    )
    keep_ref[...] = keep
    for i, copy in enumerate(large):
        copy.wait()
        for c in range(byte_dim // 128):
            wide_ref[c, PAD + i * some : PAD + (i + 1) * some, :] = x_ref[
                i * some : (i + 1) * some, c * 128 : (c + 1) * 128
            ].astype(F32)

    part = width // 8
    squares = [jnp.zeros((toks, 128), F32)]

    def conv(slot):
        for c in range(byte_dim // 128):
            cols = slice(c * 128, (c + 1) * 128)
            at = slot * byte_dim + c * 128
            here = jnp.zeros((toks, 128), F32)
            before = jnp.zeros((toks, 128), F32)
            corr = jnp.zeros((1, 128), F32)
            for tap in range(KCONV):
                weight = taps_ref[tap : tap + 1, cols]
                term = wide_ref[c, pl.ds(PAD + slot - tap, toks, stride=SHORTEN), :] * weight
                if tap > slot:
                    before = before + term
                    spot = PAD + n_bytes + slot - tap
                    corr = corr + wide_ref[c, spot : spot + 1, :] * weight
                else:
                    here = here + term
            if slot < KCONV - 1:
                here = here + before * keep_ref[0:toks, :]
                corr = corr * keep_ref[toks : toks + 1, :]
            short = here.astype(BF16)
            short_ref[:, at : at + 128] = short
            short = short.astype(F32)
            squares[0] = squares[0] + short * short
            gain = gain_ref[:, at : at + 128]
            u_ref[0:toks, at : at + 128] = (short * gain).astype(BF16)
            row = iota((EDGE, 128), 0)
            u_ref[toks:, at : at + 128] = jnp.where(row == 0, corr * gain, 0.0).astype(BF16)
            r, o = at // part, at % part
            fold_ref[8 + r : 9 + r, o : o + 128] = short[0:1]
            if slot < KCONV - 1:
                fold_ref[2 + r : 3 + r, o : o + 128] = corr

    def project(first, count):
        for group in weights[first : first + count]:
            for copy in group:
                copy.wait()
        span = slice(first * byte_dim, (first + count) * byte_dim)
        return jnp.dot(u_ref[:, span], w_ref[span, :], preferred_element_type=F32)

    middle = SHORTEN // 2
    for slot in range(middle):
        conv(slot)
    acc_ref[...] = project(0, middle)
    for slot in range(middle, SHORTEN):
        conv(slot)
    acc_ref[...] += project(middle, SHORTEN - middle)
    rs = lax.rsqrt(jnp.sum(squares[0], axis=1, keepdims=True) * (1.0 / width) + 1e-06)
    scale = jnp.where(iota((toks, 1), 0) == 0, 1.0, rs)
    out_ref[0:toks, :] = (acc_ref[0:toks, 0 : 2 * kv] * scale).astype(BF16)
    lat_ref[...] = (acc_ref[0:toks, 2 * kv :] * rs).astype(BF16)
    edge_ref[...] = acc_ref[0:8, :]
    fold_ref[0:1, :] = acc_ref[toks : toks + 1, 0 : 2 * kv]
    fold_ref[1:2, :] = jnp.concatenate(
        [acc_ref[toks : toks + 1, 2 * kv :], jnp.zeros((1, 2 * kv - rank), F32)], axis=1
    )
    out_ref[toks:, :] = fold_ref[...].astype(BF16)


def scaled_query(latent, weights):
    factor = math.log2(math.e) / math.sqrt(weights.shape[0])
    return (jnp.dot(latent, weights, preferred_element_type=F32) * factor).astype(BF16)


def plan_kernel(n_seq, rows, lens_ref, dest_ref, lat_ref, wq_ref, limit_ref, pick_ref, query_ref):
    step = min(512, wq_ref.shape[1])
    for at in range(0, wq_ref.shape[1], step):
        cols = slice(at, at + step)
        query_ref[:, cols] = scaled_query(lat_ref[...], wq_ref[:, cols])
    toks, keys = limit_ref.shape
    me = lax.axis_index("seq")
    pos = me * toks + iota((toks, 128), 0)

    def doc(d, carry):
        first, begin = carry
        return first + lens_ref[d], jnp.where(pos >= first, first, begin)

    _, begin = lax.fori_loop(
        0, lens_ref.shape[0], doc, (jnp.int32(0), jnp.zeros((toks, 128), jnp.int32))
    )
    for at in range(0, keys, 128):
        key = (me - BACK) * toks + at + iota((toks, 128), 1)
        limit_ref[:, at : at + 128] = jnp.where((key >= begin) & (key <= pos), jnp.inf, -jnp.inf)
    lane = iota((8, toks), 1)
    panel = lane // PANEL
    dest = jnp.full((8, toks), -1, jnp.int32)
    for p in range(toks // PANEL):
        dest = jnp.where(panel == p, dest_ref[p], dest)
    rank = jnp.zeros((8, toks), jnp.int32)
    for p in range(toks // PANEL):
        rank = rank + jnp.where((panel > p) & (dest == dest_ref[p]), 1, 0)
    place = (dest ^ me) * rows + rank * PANEL + lane % PANEL
    row = iota((n_seq * rows, toks), 0)
    pick_ref[...] = jnp.where(row == place[0:1], 1.0, 0.0).astype(BF16)


def put_blocks(pick, layer, refs):
    empty = (1.0 - jnp.sum(pick.astype(F32), axis=1, keepdims=True)) * MARK
    placed = (jnp.dot(pick, layer, preferred_element_type=F32) + empty).astype(BF16)
    rows = refs[0].shape[0]
    for k, ref in enumerate(refs):
        ref[...] = placed[k * rows : (k + 1) * rows]


def attend_kernel(half, batch, n_cross, query_ref, edge_ref, own_ref, one_ref, two_ref, limit_ref, pick_ref, wq_ref, short_ref, *refs):
    refs, (k_ref, v_ref, corr_ref, layer_ref) = refs[:-4], refs[-4:]
    if half == 0:
        cross_refs, out_layer_ref = refs[:-1], refs[-1]
    else:
        past_ref, refs = refs[0], refs[1:]
        cross_refs, far_refs, near_refs = refs[:n_cross], refs[n_cross : 2 * n_cross], refs[2 * n_cross :]
    toks, hd = query_ref.shape[0], k_ref.shape[1]
    wide = layer_ref.shape[1]
    heads = wide // hd
    kv = own_ref.shape[1] // 2
    part = own_ref.shape[1]
    width = 8 * part
    keys = limit_ref.shape[1]

    def root(first):
        total = jnp.sum(jnp.sum(first * first, axis=1, keepdims=True), axis=0, keepdims=True)
        return lax.rsqrt(total * (1.0 / width) + 1e-06)

    def tail(fold):
        return jnp.concatenate([fold[2:8], jnp.zeros((2, part), F32)], axis=0)

    own_fold, one_fold, two_fold = (ref[toks:, :].astype(F32) for ref in (own_ref, one_ref, two_ref))
    one_tail = tail(one_fold)
    scale = root((own_fold[8:16] + one_tail).astype(BF16).astype(F32))
    own_kv = scale * (edge_ref[0:1, 0 : 2 * kv] + one_fold[0:1])
    own_lat = scale * (edge_ref[0:1, 2 * kv :] + one_fold[1:2, 0:hd])
    scale = root((one_fold[8:16] + tail(two_fold)).astype(BF16).astype(F32))
    one_kv = scale * (one_ref[0:EDGE, :].astype(F32)[0:1] + two_fold[0:1])
    row = iota((EDGE, 2 * kv), 0)
    tops = [
        two_ref[0:EDGE, :],
        jnp.where(row == 0, one_kv, one_ref[0:EDGE, :].astype(F32)).astype(BF16),
        jnp.where(row == 0, own_kv, own_ref[0:EDGE, :].astype(F32)).astype(BF16),
    ]
    k_cols = slice(half * hd, (half + 1) * hd)
    v_cols = slice(kv + half * hd, kv + (half + 1) * hd)
    for b, ref in enumerate((two_ref, one_ref, own_ref)):
        at = b * toks
        k_ref[at : at + EDGE, :] = tops[b][:, k_cols]
        k_ref[at + EDGE : at + toks, :] = ref[EDGE:toks, k_cols]
        v_ref[at : at + EDGE, 0:hd] = tops[b][:, v_cols]
        v_ref[at + EDGE : at + toks, 0:hd] = ref[EDGE:toks, v_cols]
        v_ref[at : at + toks, hd:] = jnp.ones((toks, hd), BF16)
    for c in range(wide // part):
        at = half * (wide // part) + c
        corr_ref[:, c * part : (c + 1) * part] = one_tail[at : at + 1]
    first_lat = jnp.broadcast_to(own_lat, (EDGE, hd)).astype(BF16)
    first_query = scaled_query(first_lat, wq_ref[:, half * wide : (half + 1) * wide])
    query = query_ref[:, half * wide : (half + 1) * wide]
    top = jnp.where(iota((EDGE, wide), 0) == 0, first_query.astype(F32), query[0:EDGE].astype(F32)).astype(BF16)
    query = jnp.concatenate([top, query[EDGE:]], axis=0)
    key_all, value_all = k_ref[...], v_ref[...]
    for at in range(0, heads, batch):
        part_q = [query[:, h * hd : (h + 1) * hd] for h in range(at, at + batch)]
        scores = lax.dot_general(
            jnp.concatenate(part_q, axis=0), key_all, (((1,), (1,)), ((), ())), preferred_element_type=F32
        )
        scores = jnp.minimum(scores.reshape(batch, toks, keys), limit_ref[...][None])
        top = jnp.max(scores, axis=2, keepdims=True)
        probs = jnp.exp2(scores - top).astype(BF16).reshape(batch * toks, keys)
        mixed = jnp.dot(probs, value_all, preferred_element_type=F32)
        mixed = mixed[:, 0:hd] / mixed[:, hd:]
        for h in range(batch):
            cols = slice((at + h) * hd, (at + h + 1) * hd)
            short = short_ref[:, half * wide + (at + h) * hd : half * wide + (at + h + 1) * hd].astype(F32)
            whole = (short[0:8] + corr_ref[:, cols]).astype(BF16).astype(F32)
            first = jnp.where(iota((8, hd), 0) == 0, whole, short[0:8])
            short = jnp.concatenate([first, short[8:]], axis=0)
            layer_ref[:, cols] = (mixed[h * toks : (h + 1) * toks] + short).astype(BF16)
    middle = pick_ref.shape[0] // 2
    far = middle + middle // 2
    put_blocks(pick_ref[middle:far, :], layer_ref[...], cross_refs)
    if half == 0:
        out_layer_ref[...] = layer_ref[...]
    else:
        layer = jnp.concatenate([past_ref[...], layer_ref[...]], axis=1)
        put_blocks(pick_ref[far:, :], layer, far_refs)
        put_blocks(pick_ref[0:middle, :], layer, near_refs)


def read_parts(parts, refs, at, cols):
    return jnp.concatenate([refs[i][row : row + rows, col + at : col + at + cols] for i, row, rows, col in parts], axis=0)


def count_marks(first, block, rows, n_pad):
    used = jnp.where(rows.astype(F32) < 0.5 * MARK, 1.0, 0.0).astype(BF16)
    shape = (n_pad, rows.shape[0])
    member = iota(shape, 0) == first + iota(shape, 1) // block
    return jnp.dot(jnp.where(member, 1.0, 0.0).astype(BF16), used, preferred_element_type=F32)


def count_kernel(first, block, parts, *refs):
    count_ref = refs[-1]
    count_ref[...] = count_marks(first, block, read_parts(parts, refs, 0, 128), count_ref.shape[0])


def place_kernel(n_seq, block, near, half, parts, *refs):
    if half == 0:
        count_ref, *got_refs, out_ref, sel_ref, stage_ref, sems = refs
    else:
        sel_ref, *got_refs, _, out_ref, stage_ref, sems = refs
    pieces, toks, cols = stage_ref.shape
    if half == 0:
        me = lax.axis_index("seq")
        n_pad = count_ref.shape[0]
        n_rows = n_seq * block
        head = read_parts(parts, got_refs, 0, 128)[near * block :]
        count = count_ref[...] + count_marks(near, block, head, n_pad)
        source = me ^ iota((n_pad, 128), 0)
        offset = jnp.zeros((n_pad, 128), F32)
        for q in range(n_seq):
            offset = offset + jnp.where(source > (me ^ q), count[q : q + 1], 0.0)
        lane = iota((1, n_rows), 1)
        within = (lane % block).astype(F32)
        target = jnp.full((1, n_rows), -1.0, F32)
        for q in range(n_seq):
            valid = (lane // block == q) & (within < count[q : q + 1, 0:1])
            target = jnp.where(valid, offset[q : q + 1, 0:1] + within, target)
        sel_ref[...] = jnp.where(iota((toks, n_rows), 0).astype(F32) == target, 1.0, 0.0).astype(BF16)
    copies = []
    for i in range(pieces):
        got = read_parts(parts, got_refs, i * cols, cols)
        stage_ref[i] = jnp.dot(sel_ref[...], got, preferred_element_type=F32).astype(BF16)
        at = half * pieces * cols + i * cols
        copies.append(
            pltpu.make_async_copy(stage_ref.at[i], out_ref.at[:, pl.ds(at, cols)], sems.at[i])
        )
        copies[-1].start()
    for copy in copies:
        copy.wait()


def swap(array, by, size):
    return lax.ppermute(array, "seq", [(i, i ^ by) for i in range(size)])


def smem():
    return pl.BlockSpec(memory_space=pltpu.SMEM)


def vmem():
    return pl.BlockSpec(memory_space=pltpu.VMEM)


def hbm():
    return pl.BlockSpec(memory_space=pltpu.HBM)


def in_hbm(array):
    return pltpu.with_memory_space_constraint(array, pltpu.HBM)


def whole_block(shape):
    return pl.BlockSpec(shape, lambda i: (0,) * len(shape))


def column_block(rows, cols):
    return pl.BlockSpec((rows, cols), lambda i: (0, i))


def params(limit=32 * MIB):
    return pltpu.CompilerParams(vmem_limit_bytes=limit)


def per_device(
    byte_embed, conv_taps, norm_gain, w_qdown, w_qup, w_key, w_value, doc_lengths, panel_dest
):
    n_seq = lax.axis_size("seq")
    n_bytes, byte_dim = byte_embed.shape
    toks = n_bytes // SHORTEN
    width = SHORTEN * byte_dim
    hd = width // H
    kv = w_key.shape[1]
    kvh = kv // hd
    rank = w_qdown.shape[1]
    pans = toks // PANEL
    slots = (2 * pans + n_seq - 1) // n_seq
    rows = slots * PANEL
    merged = rows % 16 != 0
    keys = (BACK + 1) * toks
    held_rows = toks + EDGE

    held, short, latent, edge = pl.pallas_call(
        project_kernel,
        out_shape=[
            pltpu.VMEM((held_rows, 2 * kv), BF16),
            pltpu.VMEM((toks, width), BF16),
            pltpu.VMEM((toks, rank), BF16),
            pltpu.VMEM((8, 2 * kv + rank), F32),
        ],
        in_specs=[hbm()] * 7,
        out_specs=[vmem()] * 4,
        scratch_shapes=[
            pltpu.SMEM(doc_lengths.shape, jnp.int32),
            pltpu.VMEM((n_bytes, byte_dim), BF16),
            pltpu.VMEM((KCONV, byte_dim), F32),
            pltpu.VMEM((1, width), F32),
            pltpu.VMEM((width, 2 * kv + rank), BF16),
            pltpu.SemaphoreType.DMA((5,)),
            pltpu.SemaphoreType.DMA((SHORTEN, 3)),
            pltpu.VMEM((byte_dim // 128, n_bytes + 2 * PAD, 128), F32),
            pltpu.VMEM((toks + 8, 128), F32),
            pltpu.VMEM((toks + EDGE, width), BF16),
            pltpu.VMEM((toks + EDGE, 2 * kv + rank), F32),
            pltpu.VMEM((16, width // 8), F32),
        ],
        compiler_params=params(24 * MIB),
        name="project",
    )(
        *[
            in_hbm(a)
            for a in (
                doc_lengths, byte_embed, conv_taps, norm_gain.reshape(1, width), w_key, w_value, w_qdown
            )
        ]
    )

    behind = [
        lax.ppermute(held, "seq", [(i, i + by) for i in range(n_seq - by)])
        for by in range(1, BACK + 1)
    ]

    limit, pick, query = pl.pallas_call(
        functools.partial(plan_kernel, n_seq, rows),
        out_shape=[
            pltpu.VMEM((toks, keys), F32),
            pltpu.VMEM((n_seq * rows, toks), BF16),
            pltpu.VMEM((toks, width), BF16),
        ],
        in_specs=[smem()] * 2 + [vmem()] * 2,
        out_specs=[vmem()] * 3,
        compiler_params=params(),
        name="plan",
    )(doc_lengths, panel_dest, latent, w_qup)

    middle = n_seq // 2
    span = width // kvh
    def shapes(count, height, cols):
        count, height = (1, count * height) if merged else (count, height)
        return [pltpu.VMEM((height, cols), BF16)] * count

    def split(arrays, count):
        if len(arrays) == count:
            return list(arrays)
        height = arrays[0].shape[0] // count
        return [arrays[0][i * height : (i + 1) * height] for i in range(count)]

    def attend(half, outs, n_cross, more):
        operands = [query, edge, held, *behind, limit, pick, w_qup, short, *more]
        return pl.pallas_call(
            functools.partial(attend_kernel, half, BATCH[half], n_cross),
            out_shape=outs,
            in_specs=[vmem()] * len(operands),
            out_specs=[vmem()] * len(outs),
            scratch_shapes=[
                pltpu.VMEM((keys, hd), BF16),
                pltpu.VMEM((keys, 2 * hd), BF16),
                pltpu.VMEM((1, span), F32),
                pltpu.VMEM((toks, span), BF16),
            ],
            compiler_params=params(),
            name=f"attend_half_{half}",
        )(*operands)

    half_cross = middle // 2
    cross = shapes(half_cross, rows, span)
    *first, layer = attend(0, cross + [pltpu.VMEM((toks, span), BF16)], len(cross), [])
    first = split(first, half_cross)
    got_first = [swap(first[k], middle + k, n_seq) for k in range(half_cross)]
    far, near = shapes(half_cross, rows, width), shapes(middle, rows, width)
    outs = attend(1, cross + far + near, len(cross), [layer])
    second, outs = split(outs[: len(cross)], half_cross), outs[len(cross) :]
    far, near = split(outs[: len(far)], half_cross), split(outs[len(far) :], middle)
    got_far = [swap(far[k], middle + half_cross + k, n_seq) for k in range(half_cross)]
    got_near = [near[0]] + [swap(near[k], k, n_seq) for k in range(1, middle)]
    got_second = [swap(second[k], middle + k, n_seq) for k in range(half_cross)]

    def parts(found):
        if merged:
            pieces = [a[r : r + rows, c : c + span] for a, r, c in found]
            return [jnp.concatenate(pieces, axis=0)], [(0, 0, len(found) * rows, 0)]
        return [a for a, _, _ in found], [(i, r, rows, c) for i, (_, r, c) in enumerate(found)]

    near_parts = [[(a, 0, half * span) for a in got_near] for half in range(kvh)]
    cross_parts = [
        [(a, 0, 0) for a in got] + [(a, 0, half * span) for a in got_far]
        for half, got in enumerate((got_first, got_second))
    ]
    arrays, where = parts(near_parts[0])
    waits = got_first
    count = pl.pallas_call(
        functools.partial(count_kernel, 0, rows, where),
        out_shape=pltpu.VMEM((max(16, n_seq), 128), F32),
        in_specs=[vmem()] * len(arrays) + [pl.BlockSpec(memory_space=pl.ANY)] * len(waits),
        out_specs=vmem(),
        compiler_params=params(),
        name="count",
    )(*arrays, *waits)

    steps = 4
    cols = span // steps
    scratch = [pltpu.VMEM((steps, toks, cols), BF16), pltpu.SemaphoreType.DMA((steps,))]
    out_shape = jax.ShapeDtypeStruct((toks, width), BF16)
    anywhere = pl.BlockSpec(memory_space=pl.ANY)
    arrays, where = parts(near_parts[0] + cross_parts[0])
    out, sel = pl.pallas_call(
        functools.partial(place_kernel, n_seq, rows, middle, 0, where),
        out_shape=[out_shape, pltpu.VMEM((toks, n_seq * rows), BF16)],
        in_specs=[vmem()] * (1 + len(arrays)),
        out_specs=[anywhere, vmem()],
        scratch_shapes=scratch,
        compiler_params=params(),
        name="place_first",
    )(count, *arrays)
    arrays, where = parts(near_parts[1] + cross_parts[1])
    return pl.pallas_call(
        functools.partial(place_kernel, n_seq, rows, middle, 1, where),
        out_shape=out_shape,
        in_specs=[vmem()] * (1 + len(arrays)) + [anywhere],
        out_specs=anywhere,
        scratch_shapes=scratch,
        input_output_aliases={1 + len(arrays): 0},
        compiler_params=params(),
        name="place_second",
    )(sel, *arrays, out)


def solution(mesh):
    in_specs = (P(("dp", "seq"), None), P(), P(), P(), P(), P(), P(), P("dp"), P(("dp", "seq")))
    out_specs = P(("dp", "seq"), None)
    return jax.shard_map(
        per_device, mesh=mesh, in_specs=in_specs, out_specs=out_specs, check_vma=False
    )
```

```python
import functools
import math

import jax
import jax.numpy as jnp
from jax import lax
from jax.experimental import pallas as pl
from jax.experimental.pallas import tpu as pltpu
from jax.sharding import PartitionSpec as P

H = 32
SHORTEN = 4
KCONV = 4
PANEL = 4
BACK = 2
PAD = 8
EDGE = 16
MARK = 2.0**120
BATCH = (8, 4)
MIB = 1024 * 1024
F32 = jnp.float32
BF16 = jnp.bfloat16


def iota(shape, dim):
    return lax.broadcasted_iota(jnp.int32, shape, dim)


def project_kernel(
    lens_hbm, x_hbm, taps_hbm, gain_hbm, wk_hbm, wv_hbm, wd_hbm,
    out_ref, short_ref, lat_ref, edge_ref,
    lens_ref, x_ref, taps_ref, gain_ref, w_ref, sems, wsems, wide_ref, keep_ref, u_ref, acc_ref, fold_ref,
):
    n_bytes, byte_dim = x_ref.shape
    toks, width = short_ref.shape
    kv = wk_hbm.shape[1]
    rank = wd_hbm.shape[1]
    me = lax.axis_index("seq")
    pieces = 2
    some = n_bytes // pieces
    large = [
        pltpu.make_async_copy(
            x_hbm.at[pl.ds(i * some, some)], x_ref.at[pl.ds(i * some, some)], sems.at[3 + i]
        )
        for i in range(pieces)
    ]
    small = [
        pltpu.make_async_copy(lens_hbm, lens_ref, sems.at[0]),
        pltpu.make_async_copy(taps_hbm, taps_ref, sems.at[1]),
        pltpu.make_async_copy(gain_hbm, gain_ref, sems.at[2]),
    ]
    weights = []
    for i in range(SHORTEN):
        at = pl.ds(i * byte_dim, byte_dim)
        weights.append(
            [
                pltpu.make_async_copy(wk_hbm.at[at], w_ref.at[at, pl.ds(0, kv)], wsems.at[i, 0]),
                pltpu.make_async_copy(wv_hbm.at[at], w_ref.at[at, pl.ds(kv, kv)], wsems.at[i, 1]),
                pltpu.make_async_copy(wd_hbm.at[at], w_ref.at[at, pl.ds(2 * kv, rank)], wsems.at[i, 2]),
            ]
        )
    for copy in small + large:
        copy.start()
    for group in weights:
        for copy in group:
            copy.start(priority=1)
    for c in range(byte_dim // 128):
        wide_ref[c, 0:PAD, :] = jnp.zeros((PAD, 128), F32)
        wide_ref[c, PAD + n_bytes :, :] = jnp.zeros((PAD, 128), F32)
    u_ref[toks:, :] = jnp.zeros((EDGE, width), BF16)
    for copy in small:
        copy.wait()
    token = me * toks + iota((toks + 8, 128), 0)

    def doc(d, carry):
        first, keep = carry
        return first + lens_ref[d], jnp.where(token == first, 0.0, keep)

    _, keep = lax.fori_loop(
        0, lens_ref.shape[0], doc, (jnp.int32(0), jnp.ones((toks + 8, 128), F32))
    )
    keep_ref[...] = keep
    for i, copy in enumerate(large):
        copy.wait()
        for c in range(byte_dim // 128):
            wide_ref[c, PAD + i * some : PAD + (i + 1) * some, :] = x_ref[
                i * some : (i + 1) * some, c * 128 : (c + 1) * 128
            ].astype(F32)

    part = width // 8
    squares = [jnp.zeros((toks, 128), F32)]

    def conv(slot):
        for c in range(byte_dim // 128):
            cols = slice(c * 128, (c + 1) * 128)
            at = slot * byte_dim + c * 128
            here = jnp.zeros((toks, 128), F32)
            before = jnp.zeros((toks, 128), F32)
            corr = jnp.zeros((1, 128), F32)
            for tap in range(KCONV):
                weight = taps_ref[tap : tap + 1, cols]
                term = wide_ref[c, pl.ds(PAD + slot - tap, toks, stride=SHORTEN), :] * weight
                if tap > slot:
                    before = before + term
                    spot = PAD + n_bytes + slot - tap
                    corr = corr + wide_ref[c, spot : spot + 1, :] * weight
                else:
                    here = here + term
            if slot < KCONV - 1:
                here = here + before * keep_ref[0:toks, :]
                corr = corr * keep_ref[toks : toks + 1, :]
            short = here.astype(BF16)
            short_ref[:, at : at + 128] = short
            short = short.astype(F32)
            squares[0] = squares[0] + short * short
            gain = gain_ref[:, at : at + 128]
            u_ref[0:toks, at : at + 128] = (short * gain).astype(BF16)
            row = iota((EDGE, 128), 0)
            u_ref[toks:, at : at + 128] = jnp.where(row == 0, corr * gain, 0.0).astype(BF16)
            r, o = at // part, at % part
            fold_ref[8 + r : 9 + r, o : o + 128] = short[0:1]
            if slot < KCONV - 1:
                fold_ref[2 + r : 3 + r, o : o + 128] = corr

    def project(first, count):
        for group in weights[first : first + count]:
            for copy in group:
                copy.wait()
        span = slice(first * byte_dim, (first + count) * byte_dim)
        return jnp.dot(u_ref[:, span], w_ref[span, :], preferred_element_type=F32)

    middle = SHORTEN // 2
    for slot in range(middle):
        conv(slot)
    acc_ref[...] = project(0, middle)
    for slot in range(middle, SHORTEN):
        conv(slot)
    acc_ref[...] += project(middle, SHORTEN - middle)
    rs = lax.rsqrt(jnp.sum(squares[0], axis=1, keepdims=True) * (1.0 / width) + 1e-06)
    scale = jnp.where(iota((toks, 1), 0) == 0, 1.0, rs)
    out_ref[0:toks, :] = (acc_ref[0:toks, 0 : 2 * kv] * scale).astype(BF16)
    lat_ref[...] = (acc_ref[0:toks, 2 * kv :] * rs).astype(BF16)
    edge_ref[...] = acc_ref[0:8, :]
    fold_ref[0:1, :] = acc_ref[toks : toks + 1, 0 : 2 * kv]
    fold_ref[1:2, :] = jnp.concatenate(
        [acc_ref[toks : toks + 1, 2 * kv :], jnp.zeros((1, 2 * kv - rank), F32)], axis=1
    )
    out_ref[toks:, :] = fold_ref[...].astype(BF16)


def scaled_query(latent, weights):
    factor = math.log2(math.e) / math.sqrt(weights.shape[0])
    return (jnp.dot(latent, weights, preferred_element_type=F32) * factor).astype(BF16)


def plan_kernel(n_seq, rows, lens_ref, dest_ref, lat_ref, wq_ref, limit_ref, pick_ref, query_ref):
    step = min(512, wq_ref.shape[1])
    for at in range(0, wq_ref.shape[1], step):
        cols = slice(at, at + step)
        query_ref[:, cols] = scaled_query(lat_ref[...], wq_ref[:, cols])
    toks, keys = limit_ref.shape
    me = lax.axis_index("seq")
    pos = me * toks + iota((toks, 128), 0)

    def doc(d, carry):
        first, begin = carry
        return first + lens_ref[d], jnp.where(pos >= first, first, begin)

    _, begin = lax.fori_loop(
        0, lens_ref.shape[0], doc, (jnp.int32(0), jnp.zeros((toks, 128), jnp.int32))
    )
    for at in range(0, keys, 128):
        key = (me - BACK) * toks + at + iota((toks, 128), 1)
        limit_ref[:, at : at + 128] = jnp.where((key >= begin) & (key <= pos), jnp.inf, -jnp.inf)
    lane = iota((8, toks), 1)
    panel = lane // PANEL
    dest = jnp.full((8, toks), -1, jnp.int32)
    for p in range(toks // PANEL):
        dest = jnp.where(panel == p, dest_ref[p], dest)
    rank = jnp.zeros((8, toks), jnp.int32)
    for p in range(toks // PANEL):
        rank = rank + jnp.where((panel > p) & (dest == dest_ref[p]), 1, 0)
    place = (dest ^ me) * rows + rank * PANEL + lane % PANEL
    row = iota((n_seq * rows, toks), 0)
    pick_ref[...] = jnp.where(row == place[0:1], 1.0, 0.0).astype(BF16)


def put_blocks(pick, layer, refs):
    empty = (1.0 - jnp.sum(pick.astype(F32), axis=1, keepdims=True)) * MARK
    placed = (jnp.dot(pick, layer, preferred_element_type=F32) + empty).astype(BF16)
    rows = refs[0].shape[0]
    for k, ref in enumerate(refs):
        ref[...] = placed[k * rows : (k + 1) * rows]


def attend_kernel(half, batch, n_cross, query_ref, edge_ref, own_ref, one_ref, two_ref, limit_ref, pick_ref, wq_ref, short_ref, *refs):
    refs, (k_ref, v_ref, corr_ref, layer_ref) = refs[:-4], refs[-4:]
    if half == 0:
        cross_refs, out_layer_ref = refs[:-1], refs[-1]
    else:
        past_ref, refs = refs[0], refs[1:]
        cross_refs, far_refs, near_refs = refs[:n_cross], refs[n_cross : 2 * n_cross], refs[2 * n_cross :]
    toks, hd = query_ref.shape[0], k_ref.shape[1]
    wide = layer_ref.shape[1]
    heads = wide // hd
    kv = own_ref.shape[1] // 2
    part = own_ref.shape[1]
    width = 8 * part
    keys = limit_ref.shape[1]

    def root(first):
        total = jnp.sum(jnp.sum(first * first, axis=1, keepdims=True), axis=0, keepdims=True)
        return lax.rsqrt(total * (1.0 / width) + 1e-06)

    def tail(fold):
        return jnp.concatenate([fold[2:8], jnp.zeros((2, part), F32)], axis=0)

    own_fold, one_fold, two_fold = (ref[toks:, :].astype(F32) for ref in (own_ref, one_ref, two_ref))
    one_tail = tail(one_fold)
    scale = root((own_fold[8:16] + one_tail).astype(BF16).astype(F32))
    own_kv = scale * (edge_ref[0:1, 0 : 2 * kv] + one_fold[0:1])
    own_lat = scale * (edge_ref[0:1, 2 * kv :] + one_fold[1:2, 0:hd])
    scale = root((one_fold[8:16] + tail(two_fold)).astype(BF16).astype(F32))
    one_kv = scale * (one_ref[0:EDGE, :].astype(F32)[0:1] + two_fold[0:1])
    row = iota((EDGE, 2 * kv), 0)
    tops = [
        two_ref[0:EDGE, :],
        jnp.where(row == 0, one_kv, one_ref[0:EDGE, :].astype(F32)).astype(BF16),
        jnp.where(row == 0, own_kv, own_ref[0:EDGE, :].astype(F32)).astype(BF16),
    ]
    k_cols = slice(half * hd, (half + 1) * hd)
    v_cols = slice(kv + half * hd, kv + (half + 1) * hd)
    for b, ref in enumerate((two_ref, one_ref, own_ref)):
        at = b * toks
        k_ref[at : at + EDGE, :] = tops[b][:, k_cols]
        k_ref[at + EDGE : at + toks, :] = ref[EDGE:toks, k_cols]
        v_ref[at : at + EDGE, 0:hd] = tops[b][:, v_cols]
        v_ref[at + EDGE : at + toks, 0:hd] = ref[EDGE:toks, v_cols]
        v_ref[at : at + toks, hd:] = jnp.ones((toks, hd), BF16)
    for c in range(wide // part):
        at = half * (wide // part) + c
        corr_ref[:, c * part : (c + 1) * part] = one_tail[at : at + 1]
    first_lat = jnp.broadcast_to(own_lat, (EDGE, hd)).astype(BF16)
    first_query = scaled_query(first_lat, wq_ref[:, half * wide : (half + 1) * wide])
    query = query_ref[:, half * wide : (half + 1) * wide]
    top = jnp.where(iota((EDGE, wide), 0) == 0, first_query.astype(F32), query[0:EDGE].astype(F32)).astype(BF16)
    query = jnp.concatenate([top, query[EDGE:]], axis=0)
    key_all, value_all = k_ref[...], v_ref[...]
    for at in range(0, heads, batch):
        part_q = [query[:, h * hd : (h + 1) * hd] for h in range(at, at + batch)]
        scores = lax.dot_general(
            jnp.concatenate(part_q, axis=0), key_all, (((1,), (1,)), ((), ())), preferred_element_type=F32
        )
        scores = jnp.minimum(scores.reshape(batch, toks, keys), limit_ref[...][None])
        top = jnp.max(scores, axis=2, keepdims=True)
        probs = jnp.exp2(scores - top).astype(BF16).reshape(batch * toks, keys)
        mixed = jnp.dot(probs, value_all, preferred_element_type=F32)
        mixed = mixed[:, 0:hd] / mixed[:, hd:]
        for h in range(batch):
            cols = slice((at + h) * hd, (at + h + 1) * hd)
            short = short_ref[:, half * wide + (at + h) * hd : half * wide + (at + h + 1) * hd].astype(F32)
            whole = (short[0:8] + corr_ref[:, cols]).astype(BF16).astype(F32)
            first = jnp.where(iota((8, hd), 0) == 0, whole, short[0:8])
            short = jnp.concatenate([first, short[8:]], axis=0)
            layer_ref[:, cols] = (mixed[h * toks : (h + 1) * toks] + short).astype(BF16)
    middle = pick_ref.shape[0] // 2
    far = middle + middle // 2
    put_blocks(pick_ref[far:, :], layer_ref[...], cross_refs)
    if half == 0:
        out_layer_ref[...] = layer_ref[...]
    else:
        layer = jnp.concatenate([past_ref[...], layer_ref[...]], axis=1)
        put_blocks(pick_ref[middle:far, :], layer, far_refs)
        put_blocks(pick_ref[0:middle, :], layer, near_refs)


def read_parts(parts, refs, at, cols):
    return jnp.concatenate([refs[i][row : row + rows, col + at : col + at + cols] for i, row, rows, col in parts], axis=0)


def count_marks(first, block, rows, n_pad):
    used = jnp.where(rows.astype(F32) < 0.5 * MARK, 1.0, 0.0).astype(BF16)
    shape = (n_pad, rows.shape[0])
    member = iota(shape, 0) == first + iota(shape, 1) // block
    return jnp.dot(jnp.where(member, 1.0, 0.0).astype(BF16), used, preferred_element_type=F32)


def count_kernel(first, block, parts, *refs):
    count_ref = refs[-1]
    count_ref[...] = count_marks(first, block, read_parts(parts, refs, 0, 128), count_ref.shape[0])


def place_kernel(n_seq, block, near, half, parts, *refs):
    if half == 0:
        count_ref, *got_refs, out_ref, sel_ref, stage_ref, sems = refs
    else:
        sel_ref, *got_refs, _, out_ref, stage_ref, sems = refs
    pieces, toks, cols = stage_ref.shape
    if half == 0:
        me = lax.axis_index("seq")
        n_pad = count_ref.shape[0]
        n_rows = n_seq * block
        head = read_parts(parts, got_refs, 0, 128)[near * block :]
        count = count_ref[...] + count_marks(near, block, head, n_pad)
        source = me ^ iota((n_pad, 128), 0)
        offset = jnp.zeros((n_pad, 128), F32)
        for q in range(n_seq):
            offset = offset + jnp.where(source > (me ^ q), count[q : q + 1], 0.0)
        lane = iota((1, n_rows), 1)
        within = (lane % block).astype(F32)
        target = jnp.full((1, n_rows), -1.0, F32)
        for q in range(n_seq):
            valid = (lane // block == q) & (within < count[q : q + 1, 0:1])
            target = jnp.where(valid, offset[q : q + 1, 0:1] + within, target)
        sel_ref[...] = jnp.where(iota((toks, n_rows), 0).astype(F32) == target, 1.0, 0.0).astype(BF16)
    copies = []
    for i in range(pieces):
        got = read_parts(parts, got_refs, i * cols, cols)
        stage_ref[i] = jnp.dot(sel_ref[...], got, preferred_element_type=F32).astype(BF16)
        at = half * pieces * cols + i * cols
        copies.append(
            pltpu.make_async_copy(stage_ref.at[i], out_ref.at[:, pl.ds(at, cols)], sems.at[i])
        )
        copies[-1].start()
    for copy in copies:
        copy.wait()


def swap(array, by, size):
    return lax.ppermute(array, "seq", [(i, i ^ by) for i in range(size)])


def smem():
    return pl.BlockSpec(memory_space=pltpu.SMEM)


def vmem():
    return pl.BlockSpec(memory_space=pltpu.VMEM)


def hbm():
    return pl.BlockSpec(memory_space=pltpu.HBM)


def in_hbm(array):
    return pltpu.with_memory_space_constraint(array, pltpu.HBM)


def whole_block(shape):
    return pl.BlockSpec(shape, lambda i: (0,) * len(shape))


def column_block(rows, cols):
    return pl.BlockSpec((rows, cols), lambda i: (0, i))


def params(limit=32 * MIB):
    return pltpu.CompilerParams(vmem_limit_bytes=limit)


def per_device(
    byte_embed, conv_taps, norm_gain, w_qdown, w_qup, w_key, w_value, doc_lengths, panel_dest
):
    n_seq = lax.axis_size("seq")
    n_bytes, byte_dim = byte_embed.shape
    toks = n_bytes // SHORTEN
    width = SHORTEN * byte_dim
    hd = width // H
    kv = w_key.shape[1]
    kvh = kv // hd
    rank = w_qdown.shape[1]
    pans = toks // PANEL
    slots = (2 * pans + n_seq - 1) // n_seq
    rows = slots * PANEL
    merged = rows % 16 != 0
    keys = (BACK + 1) * toks
    held_rows = toks + EDGE

    held, short, latent, edge = pl.pallas_call(
        project_kernel,
        out_shape=[
            pltpu.VMEM((held_rows, 2 * kv), BF16),
            pltpu.VMEM((toks, width), BF16),
            pltpu.VMEM((toks, rank), BF16),
            pltpu.VMEM((8, 2 * kv + rank), F32),
        ],
        in_specs=[hbm()] * 7,
        out_specs=[vmem()] * 4,
        scratch_shapes=[
            pltpu.SMEM(doc_lengths.shape, jnp.int32),
            pltpu.VMEM((n_bytes, byte_dim), BF16),
            pltpu.VMEM((KCONV, byte_dim), F32),
            pltpu.VMEM((1, width), F32),
            pltpu.VMEM((width, 2 * kv + rank), BF16),
            pltpu.SemaphoreType.DMA((5,)),
            pltpu.SemaphoreType.DMA((SHORTEN, 3)),
            pltpu.VMEM((byte_dim // 128, n_bytes + 2 * PAD, 128), F32),
            pltpu.VMEM((toks + 8, 128), F32),
            pltpu.VMEM((toks + EDGE, width), BF16),
            pltpu.VMEM((toks + EDGE, 2 * kv + rank), F32),
            pltpu.VMEM((16, width // 8), F32),
        ],
        compiler_params=params(24 * MIB),
        name="project",
    )(
        *[
            in_hbm(a)
            for a in (
                doc_lengths, byte_embed, conv_taps, norm_gain.reshape(1, width), w_key, w_value, w_qdown
            )
        ]
    )

    behind = [
        lax.ppermute(held, "seq", [(i, i + by) for i in range(n_seq - by)])
        for by in range(1, BACK + 1)
    ]

    limit, pick, query = pl.pallas_call(
        functools.partial(plan_kernel, n_seq, rows),
        out_shape=[
            pltpu.VMEM((toks, keys), F32),
            pltpu.VMEM((n_seq * rows, toks), BF16),
            pltpu.VMEM((toks, width), BF16),
        ],
        in_specs=[smem()] * 2 + [vmem()] * 2,
        out_specs=[vmem()] * 3,
        compiler_params=params(),
        name="plan",
    )(doc_lengths, panel_dest, latent, w_qup)

    middle = n_seq // 2
    span = width // kvh
    def shapes(count, height, cols):
        count, height = (1, count * height) if merged else (count, height)
        return [pltpu.VMEM((height, cols), BF16)] * count

    def split(arrays, count):
        if len(arrays) == count:
            return list(arrays)
        height = arrays[0].shape[0] // count
        return [arrays[0][i * height : (i + 1) * height] for i in range(count)]

    def attend(half, outs, n_cross, more):
        operands = [query, edge, held, *behind, limit, pick, w_qup, short, *more]
        return pl.pallas_call(
            functools.partial(attend_kernel, half, BATCH[half], n_cross),
            out_shape=outs,
            in_specs=[vmem()] * len(operands),
            out_specs=[vmem()] * len(outs),
            scratch_shapes=[
                pltpu.VMEM((keys, hd), BF16),
                pltpu.VMEM((keys, 2 * hd), BF16),
                pltpu.VMEM((1, span), F32),
                pltpu.VMEM((toks, span), BF16),
            ],
            compiler_params=params(),
            name=f"attend_half_{half}",
        )(*operands)

    half_cross = middle // 2
    cross = shapes(half_cross, rows, span)
    *first, layer = attend(0, cross + [pltpu.VMEM((toks, span), BF16)], len(cross), [])
    first = split(first, half_cross)
    got_first = [swap(first[k], middle + half_cross + k, n_seq) for k in range(half_cross)]
    far, near = shapes(half_cross, rows, width), shapes(middle, rows, width)
    outs = attend(1, cross + far + near, len(cross), [layer])
    second, outs = split(outs[: len(cross)], half_cross), outs[len(cross) :]
    far, near = split(outs[: len(far)], half_cross), split(outs[len(far) :], middle)
    got_far = [swap(far[k], middle + k, n_seq) for k in range(half_cross)]
    got_near = [near[0]] + [swap(near[k], k, n_seq) for k in range(1, middle)]
    got_second = [swap(second[k], middle + half_cross + k, n_seq) for k in range(half_cross)]

    def parts(found):
        if merged:
            pieces = [a[r : r + rows, c : c + span] for a, r, c in found]
            return [jnp.concatenate(pieces, axis=0)], [(0, 0, len(found) * rows, 0)]
        return [a for a, _, _ in found], [(i, r, rows, c) for i, (_, r, c) in enumerate(found)]

    near_parts = [[(a, 0, half * span) for a in got_near] for half in range(kvh)]
    cross_parts = [
        [(a, 0, half * span) for a in got_far] + [(a, 0, 0) for a in got]
        for half, got in enumerate((got_first, got_second))
    ]
    arrays, where = parts(near_parts[0])
    waits = got_first
    count = pl.pallas_call(
        functools.partial(count_kernel, 0, rows, where),
        out_shape=pltpu.VMEM((max(16, n_seq), 128), F32),
        in_specs=[vmem()] * len(arrays) + [pl.BlockSpec(memory_space=pl.ANY)] * len(waits),
        out_specs=vmem(),
        compiler_params=params(),
        name="count",
    )(*arrays, *waits)

    steps = 4
    cols = span // steps
    scratch = [pltpu.VMEM((steps, toks, cols), BF16), pltpu.SemaphoreType.DMA((steps,))]
    out_shape = jax.ShapeDtypeStruct((toks, width), BF16)
    anywhere = pl.BlockSpec(memory_space=pl.ANY)
    arrays, where = parts(near_parts[0] + cross_parts[0])
    out, sel = pl.pallas_call(
        functools.partial(place_kernel, n_seq, rows, middle, 0, where),
        out_shape=[out_shape, pltpu.VMEM((toks, n_seq * rows), BF16)],
        in_specs=[vmem()] * (1 + len(arrays)),
        out_specs=[anywhere, vmem()],
        scratch_shapes=scratch,
        compiler_params=params(),
        name="place_first",
    )(count, *arrays)
    arrays, where = parts(near_parts[1] + cross_parts[1])
    return pl.pallas_call(
        functools.partial(place_kernel, n_seq, rows, middle, 1, where),
        out_shape=out_shape,
        in_specs=[vmem()] * (1 + len(arrays)) + [anywhere],
        out_specs=anywhere,
        scratch_shapes=scratch,
        input_output_aliases={1 + len(arrays): 0},
        compiler_params=params(),
        name="place_second",
    )(sel, *arrays, out)


def solution(mesh):
    in_specs = (P(("dp", "seq"), None), P(), P(), P(), P(), P(), P(), P("dp"), P(("dp", "seq")))
    out_specs = P(("dp", "seq"), None)
    return jax.shard_map(
        per_device, mesh=mesh, in_specs=in_specs, out_specs=out_specs, check_vma=False
    )
```

```python
import functools
import math

import jax
import jax.numpy as jnp
from jax import lax
from jax.experimental import pallas as pl
from jax.experimental.pallas import tpu as pltpu
from jax.sharding import PartitionSpec as P

H = 32
SHORTEN = 4
KCONV = 4
PANEL = 4
BACK = 2
PAD = 8
EDGE = 16
MARK = 2.0**120
BATCH = (8, 4)
MIB = 1024 * 1024
F32 = jnp.float32
BF16 = jnp.bfloat16


def iota(shape, dim):
    return lax.broadcasted_iota(jnp.int32, shape, dim)


def project_kernel(
    lens_hbm, x_hbm, taps_hbm, gain_hbm, wk_hbm, wv_hbm, wd_hbm,
    out_ref, short_ref, lat_ref, edge_ref,
    lens_ref, x_ref, taps_ref, gain_ref, w_ref, sems, wsems, wide_ref, keep_ref, u_ref, acc_ref, fold_ref,
):
    n_bytes, byte_dim = x_ref.shape
    toks, width = short_ref.shape
    kv = wk_hbm.shape[1]
    rank = wd_hbm.shape[1]
    me = lax.axis_index("seq")
    pieces = 2
    some = n_bytes // pieces
    large = [
        pltpu.make_async_copy(
            x_hbm.at[pl.ds(i * some, some)], x_ref.at[pl.ds(i * some, some)], sems.at[3 + i]
        )
        for i in range(pieces)
    ]
    small = [
        pltpu.make_async_copy(lens_hbm, lens_ref, sems.at[0]),
        pltpu.make_async_copy(taps_hbm, taps_ref, sems.at[1]),
        pltpu.make_async_copy(gain_hbm, gain_ref, sems.at[2]),
    ]
    weights = []
    for i in range(SHORTEN):
        at = pl.ds(i * byte_dim, byte_dim)
        weights.append(
            [
                pltpu.make_async_copy(wk_hbm.at[at], w_ref.at[at, pl.ds(0, kv)], wsems.at[i, 0]),
                pltpu.make_async_copy(wv_hbm.at[at], w_ref.at[at, pl.ds(kv, kv)], wsems.at[i, 1]),
                pltpu.make_async_copy(wd_hbm.at[at], w_ref.at[at, pl.ds(2 * kv, rank)], wsems.at[i, 2]),
            ]
        )
    for copy in small + large:
        copy.start()
    for group in weights:
        for copy in group:
            copy.start(priority=1)
    for c in range(byte_dim // 128):
        wide_ref[c, 0:PAD, :] = jnp.zeros((PAD, 128), F32)
        wide_ref[c, PAD + n_bytes :, :] = jnp.zeros((PAD, 128), F32)
    u_ref[toks:, :] = jnp.zeros((EDGE, width), BF16)
    for copy in small:
        copy.wait()
    token = me * toks + iota((toks + 8, 128), 0)

    def doc(d, carry):
        first, keep = carry
        return first + lens_ref[d], jnp.where(token == first, 0.0, keep)

    _, keep = lax.fori_loop(
        0, lens_ref.shape[0], doc, (jnp.int32(0), jnp.ones((toks + 8, 128), F32))
    )
    keep_ref[...] = keep
    for i, copy in enumerate(large):
        copy.wait()
        for c in range(byte_dim // 128):
            wide_ref[c, PAD + i * some : PAD + (i + 1) * some, :] = x_ref[
                i * some : (i + 1) * some, c * 128 : (c + 1) * 128
            ].astype(F32)

    part = width // 8
    squares = [jnp.zeros((toks, 128), F32)]

    def conv(slot):
        for c in range(byte_dim // 128):
            cols = slice(c * 128, (c + 1) * 128)
            at = slot * byte_dim + c * 128
            here = jnp.zeros((toks, 128), F32)
            before = jnp.zeros((toks, 128), F32)
            corr = jnp.zeros((1, 128), F32)
            for tap in range(KCONV):
                weight = taps_ref[tap : tap + 1, cols]
                term = wide_ref[c, pl.ds(PAD + slot - tap, toks, stride=SHORTEN), :] * weight
                if tap > slot:
                    before = before + term
                    spot = PAD + n_bytes + slot - tap
                    corr = corr + wide_ref[c, spot : spot + 1, :] * weight
                else:
                    here = here + term
            if slot < KCONV - 1:
                here = here + before * keep_ref[0:toks, :]
                corr = corr * keep_ref[toks : toks + 1, :]
            short = here.astype(BF16)
            short_ref[:, at : at + 128] = short
            short = short.astype(F32)
            squares[0] = squares[0] + short * short
            gain = gain_ref[:, at : at + 128]
            u_ref[0:toks, at : at + 128] = (short * gain).astype(BF16)
            row = iota((EDGE, 128), 0)
            u_ref[toks:, at : at + 128] = jnp.where(row == 0, corr * gain, 0.0).astype(BF16)
            r, o = at // part, at % part
            fold_ref[8 + r : 9 + r, o : o + 128] = short[0:1]
            if slot < KCONV - 1:
                fold_ref[2 + r : 3 + r, o : o + 128] = corr

    def project(first, count):
        for group in weights[first : first + count]:
            for copy in group:
                copy.wait()
        span = slice(first * byte_dim, (first + count) * byte_dim)
        return jnp.dot(u_ref[:, span], w_ref[span, :], preferred_element_type=F32)

    middle = SHORTEN // 2
    for slot in range(middle):
        conv(slot)
    acc_ref[...] = project(0, middle)
    for slot in range(middle, SHORTEN):
        conv(slot)
    acc_ref[...] += project(middle, SHORTEN - middle)
    rs = lax.rsqrt(jnp.sum(squares[0], axis=1, keepdims=True) * (1.0 / width) + 1e-06)
    scale = jnp.where(iota((toks, 1), 0) == 0, 1.0, rs)
    out_ref[0:toks, :] = (acc_ref[0:toks, 0 : 2 * kv] * scale).astype(BF16)
    lat_ref[...] = (acc_ref[0:toks, 2 * kv :] * rs).astype(BF16)
    edge_ref[...] = acc_ref[0:8, :]
    fold_ref[0:1, :] = acc_ref[toks : toks + 1, 0 : 2 * kv]
    fold_ref[1:2, :] = jnp.concatenate(
        [acc_ref[toks : toks + 1, 2 * kv :], jnp.zeros((1, 2 * kv - rank), F32)], axis=1
    )
    out_ref[toks:, :] = fold_ref[...].astype(BF16)


def scaled_query(latent, weights):
    factor = math.log2(math.e) / math.sqrt(weights.shape[0])
    return (jnp.dot(latent, weights, preferred_element_type=F32) * factor).astype(BF16)


def plan_kernel(n_seq, rows, lens_ref, dest_ref, lat_ref, wq_ref, limit_ref, pick_ref, query_ref):
    step = min(512, wq_ref.shape[1])
    for at in range(0, wq_ref.shape[1], step):
        cols = slice(at, at + step)
        query_ref[:, cols] = scaled_query(lat_ref[...], wq_ref[:, cols])
    toks, keys = limit_ref.shape
    me = lax.axis_index("seq")
    pos = me * toks + iota((toks, 128), 0)

    def doc(d, carry):
        first, begin = carry
        return first + lens_ref[d], jnp.where(pos >= first, first, begin)

    _, begin = lax.fori_loop(
        0, lens_ref.shape[0], doc, (jnp.int32(0), jnp.zeros((toks, 128), jnp.int32))
    )
    for at in range(0, keys, 128):
        key = (me - BACK) * toks + at + iota((toks, 128), 1)
        limit_ref[:, at : at + 128] = jnp.where((key >= begin) & (key <= pos), jnp.inf, -jnp.inf)
    lane = iota((8, toks), 1)
    panel = lane // PANEL
    dest = jnp.full((8, toks), -1, jnp.int32)
    for p in range(toks // PANEL):
        dest = jnp.where(panel == p, dest_ref[p], dest)
    rank = jnp.zeros((8, toks), jnp.int32)
    for p in range(toks // PANEL):
        rank = rank + jnp.where((panel > p) & (dest == dest_ref[p]), 1, 0)
    place = (dest ^ me) * rows + rank * PANEL + lane % PANEL
    row = iota((n_seq * rows, toks), 0)
    pick_ref[...] = jnp.where(row == place[0:1], 1.0, 0.0).astype(BF16)


def put_blocks(pick, layer, refs):
    empty = (1.0 - jnp.sum(pick.astype(F32), axis=1, keepdims=True)) * MARK
    placed = (jnp.dot(pick, layer, preferred_element_type=F32) + empty).astype(BF16)
    rows = refs[0].shape[0]
    for k, ref in enumerate(refs):
        ref[...] = placed[k * rows : (k + 1) * rows]


def attend_kernel(half, batch, n_cross, query_ref, edge_ref, own_ref, two_ref, one_ref, limit_ref, pick_ref, wq_ref, short_ref, *refs):
    refs, (k_ref, v_ref, corr_ref, layer_ref) = refs[:-4], refs[-4:]
    if half == 0:
        cross_refs, out_layer_ref = refs[:-1], refs[-1]
    else:
        past_ref, refs = refs[0], refs[1:]
        cross_refs, far_refs, near_refs = refs[:n_cross], refs[n_cross : 2 * n_cross], refs[2 * n_cross :]
    toks, hd = query_ref.shape[0], k_ref.shape[1]
    wide = layer_ref.shape[1]
    heads = wide // hd
    kv = own_ref.shape[1] // 2
    part = own_ref.shape[1]
    width = 8 * part
    keys = limit_ref.shape[1]

    def root(first):
        total = jnp.sum(jnp.sum(first * first, axis=1, keepdims=True), axis=0, keepdims=True)
        return lax.rsqrt(total * (1.0 / width) + 1e-06)

    def tail(fold):
        return jnp.concatenate([fold[2:8], jnp.zeros((2, part), F32)], axis=0)

    own_fold, one_fold, two_fold = (ref[toks:, :].astype(F32) for ref in (own_ref, one_ref, two_ref))
    one_tail = tail(one_fold)
    scale = root((own_fold[8:16] + one_tail).astype(BF16).astype(F32))
    own_kv = scale * (edge_ref[0:1, 0 : 2 * kv] + one_fold[0:1])
    own_lat = scale * (edge_ref[0:1, 2 * kv :] + one_fold[1:2, 0:hd])
    scale = root((one_fold[8:16] + tail(two_fold)).astype(BF16).astype(F32))
    one_kv = scale * (one_ref[0:EDGE, :].astype(F32)[0:1] + two_fold[0:1])
    row = iota((EDGE, 2 * kv), 0)
    tops = [
        two_ref[0:EDGE, :],
        jnp.where(row == 0, one_kv, one_ref[0:EDGE, :].astype(F32)).astype(BF16),
        jnp.where(row == 0, own_kv, own_ref[0:EDGE, :].astype(F32)).astype(BF16),
    ]
    k_cols = slice(half * hd, (half + 1) * hd)
    v_cols = slice(kv + half * hd, kv + (half + 1) * hd)
    for b, ref in enumerate((two_ref, one_ref, own_ref)):
        at = b * toks
        k_ref[at : at + EDGE, :] = tops[b][:, k_cols]
        k_ref[at + EDGE : at + toks, :] = ref[EDGE:toks, k_cols]
        v_ref[at : at + EDGE, 0:hd] = tops[b][:, v_cols]
        v_ref[at + EDGE : at + toks, 0:hd] = ref[EDGE:toks, v_cols]
        v_ref[at : at + toks, hd:] = jnp.ones((toks, hd), BF16)
    for c in range(wide // part):
        at = half * (wide // part) + c
        corr_ref[:, c * part : (c + 1) * part] = one_tail[at : at + 1]
    first_lat = jnp.broadcast_to(own_lat, (EDGE, hd)).astype(BF16)
    first_query = scaled_query(first_lat, wq_ref[:, half * wide : (half + 1) * wide])
    query = query_ref[:, half * wide : (half + 1) * wide]
    top = jnp.where(iota((EDGE, wide), 0) == 0, first_query.astype(F32), query[0:EDGE].astype(F32)).astype(BF16)
    query = jnp.concatenate([top, query[EDGE:]], axis=0)
    key_all, value_all = k_ref[...], v_ref[...]
    for at in range(0, heads, batch):
        part_q = [query[:, h * hd : (h + 1) * hd] for h in range(at, at + batch)]
        scores = lax.dot_general(
            jnp.concatenate(part_q, axis=0), key_all, (((1,), (1,)), ((), ())), preferred_element_type=F32
        )
        scores = jnp.minimum(scores.reshape(batch, toks, keys), limit_ref[...][None])
        top = jnp.max(scores, axis=2, keepdims=True)
        probs = jnp.exp2(scores - top).astype(BF16).reshape(batch * toks, keys)
        mixed = jnp.dot(probs, value_all, preferred_element_type=F32)
        mixed = mixed[:, 0:hd] / mixed[:, hd:]
        for h in range(batch):
            cols = slice((at + h) * hd, (at + h + 1) * hd)
            short = short_ref[:, half * wide + (at + h) * hd : half * wide + (at + h + 1) * hd].astype(F32)
            whole = (short[0:8] + corr_ref[:, cols]).astype(BF16).astype(F32)
            first = jnp.where(iota((8, hd), 0) == 0, whole, short[0:8])
            short = jnp.concatenate([first, short[8:]], axis=0)
            layer_ref[:, cols] = (mixed[h * toks : (h + 1) * toks] + short).astype(BF16)
    middle = pick_ref.shape[0] // 2
    far = middle + middle // 2
    put_blocks(pick_ref[far:, :], layer_ref[...], cross_refs)
    if half == 0:
        out_layer_ref[...] = layer_ref[...]
    else:
        layer = jnp.concatenate([past_ref[...], layer_ref[...]], axis=1)
        put_blocks(pick_ref[middle:far, :], layer, far_refs)
        put_blocks(pick_ref[0:middle, :], layer, near_refs)


def read_parts(parts, refs, at, cols):
    return jnp.concatenate([refs[i][row : row + rows, col + at : col + at + cols] for i, row, rows, col in parts], axis=0)


def count_marks(first, block, rows, n_pad):
    used = jnp.where(rows.astype(F32) < 0.5 * MARK, 1.0, 0.0).astype(BF16)
    shape = (n_pad, rows.shape[0])
    member = iota(shape, 0) == first + iota(shape, 1) // block
    return jnp.dot(jnp.where(member, 1.0, 0.0).astype(BF16), used, preferred_element_type=F32)


def count_kernel(first, block, parts, *refs):
    count_ref = refs[-1]
    count_ref[...] = count_marks(first, block, read_parts(parts, refs, 0, 128), count_ref.shape[0])


def place_kernel(n_seq, block, near, half, parts, *refs):
    if half == 0:
        count_ref, *got_refs, out_ref, sel_ref, stage_ref, sems = refs
    else:
        sel_ref, *got_refs, _, out_ref, stage_ref, sems = refs
    pieces, toks, cols = stage_ref.shape
    if half == 0:
        me = lax.axis_index("seq")
        n_pad = count_ref.shape[0]
        n_rows = n_seq * block
        head = read_parts(parts, got_refs, 0, 128)[near * block :]
        count = count_ref[...] + count_marks(near, block, head, n_pad)
        source = me ^ iota((n_pad, 128), 0)
        offset = jnp.zeros((n_pad, 128), F32)
        for q in range(n_seq):
            offset = offset + jnp.where(source > (me ^ q), count[q : q + 1], 0.0)
        lane = iota((1, n_rows), 1)
        within = (lane % block).astype(F32)
        target = jnp.full((1, n_rows), -1.0, F32)
        for q in range(n_seq):
            valid = (lane // block == q) & (within < count[q : q + 1, 0:1])
            target = jnp.where(valid, offset[q : q + 1, 0:1] + within, target)
        sel_ref[...] = jnp.where(iota((toks, n_rows), 0).astype(F32) == target, 1.0, 0.0).astype(BF16)
    copies = []
    for i in range(pieces):
        got = read_parts(parts, got_refs, i * cols, cols)
        stage_ref[i] = jnp.dot(sel_ref[...], got, preferred_element_type=F32).astype(BF16)
        at = half * pieces * cols + i * cols
        copies.append(
            pltpu.make_async_copy(stage_ref.at[i], out_ref.at[:, pl.ds(at, cols)], sems.at[i])
        )
        copies[-1].start()
    for copy in copies:
        copy.wait()


def swap(array, by, size):
    return lax.ppermute(array, "seq", [(i, i ^ by) for i in range(size)])


def smem():
    return pl.BlockSpec(memory_space=pltpu.SMEM)


def vmem():
    return pl.BlockSpec(memory_space=pltpu.VMEM)


def hbm():
    return pl.BlockSpec(memory_space=pltpu.HBM)


def in_hbm(array):
    return pltpu.with_memory_space_constraint(array, pltpu.HBM)


def whole_block(shape):
    return pl.BlockSpec(shape, lambda i: (0,) * len(shape))


def column_block(rows, cols):
    return pl.BlockSpec((rows, cols), lambda i: (0, i))


def params(limit=32 * MIB):
    return pltpu.CompilerParams(vmem_limit_bytes=limit)


def per_device(
    byte_embed, conv_taps, norm_gain, w_qdown, w_qup, w_key, w_value, doc_lengths, panel_dest
):
    n_seq = lax.axis_size("seq")
    n_bytes, byte_dim = byte_embed.shape
    toks = n_bytes // SHORTEN
    width = SHORTEN * byte_dim
    hd = width // H
    kv = w_key.shape[1]
    kvh = kv // hd
    rank = w_qdown.shape[1]
    pans = toks // PANEL
    slots = (2 * pans + n_seq - 1) // n_seq
    rows = slots * PANEL
    merged = rows % 16 != 0
    keys = (BACK + 1) * toks
    held_rows = toks + EDGE

    held, short, latent, edge = pl.pallas_call(
        project_kernel,
        out_shape=[
            pltpu.VMEM((held_rows, 2 * kv), BF16),
            pltpu.VMEM((toks, width), BF16),
            pltpu.VMEM((toks, rank), BF16),
            pltpu.VMEM((8, 2 * kv + rank), F32),
        ],
        in_specs=[hbm()] * 7,
        out_specs=[vmem()] * 4,
        scratch_shapes=[
            pltpu.SMEM(doc_lengths.shape, jnp.int32),
            pltpu.VMEM((n_bytes, byte_dim), BF16),
            pltpu.VMEM((KCONV, byte_dim), F32),
            pltpu.VMEM((1, width), F32),
            pltpu.VMEM((width, 2 * kv + rank), BF16),
            pltpu.SemaphoreType.DMA((5,)),
            pltpu.SemaphoreType.DMA((SHORTEN, 3)),
            pltpu.VMEM((byte_dim // 128, n_bytes + 2 * PAD, 128), F32),
            pltpu.VMEM((toks + 8, 128), F32),
            pltpu.VMEM((toks + EDGE, width), BF16),
            pltpu.VMEM((toks + EDGE, 2 * kv + rank), F32),
            pltpu.VMEM((16, width // 8), F32),
        ],
        compiler_params=params(24 * MIB),
        name="project",
    )(
        *[
            in_hbm(a)
            for a in (
                doc_lengths, byte_embed, conv_taps, norm_gain.reshape(1, width), w_key, w_value, w_qdown
            )
        ]
    )

    behind = [
        lax.ppermute(held, "seq", [(i, i + by) for i in range(n_seq - by)])
        for by in range(1, BACK + 1)
    ]

    limit, pick, query = pl.pallas_call(
        functools.partial(plan_kernel, n_seq, rows),
        out_shape=[
            pltpu.VMEM((toks, keys), F32),
            pltpu.VMEM((n_seq * rows, toks), BF16),
            pltpu.VMEM((toks, width), BF16),
        ],
        in_specs=[smem()] * 2 + [vmem()] * 2,
        out_specs=[vmem()] * 3,
        compiler_params=params(),
        name="plan",
    )(doc_lengths, panel_dest, latent, w_qup)

    middle = n_seq // 2
    span = width // kvh
    def shapes(count, height, cols):
        count, height = (1, count * height) if merged else (count, height)
        return [pltpu.VMEM((height, cols), BF16)] * count

    def split(arrays, count):
        if len(arrays) == count:
            return list(arrays)
        height = arrays[0].shape[0] // count
        return [arrays[0][i * height : (i + 1) * height] for i in range(count)]

    def attend(half, outs, n_cross, more):
        operands = [query, edge, held, *behind[::-1], limit, pick, w_qup, short, *more]
        return pl.pallas_call(
            functools.partial(attend_kernel, half, BATCH[half], n_cross),
            out_shape=outs,
            in_specs=[vmem()] * len(operands),
            out_specs=[vmem()] * len(outs),
            scratch_shapes=[
                pltpu.VMEM((keys, hd), BF16),
                pltpu.VMEM((keys, 2 * hd), BF16),
                pltpu.VMEM((1, span), F32),
                pltpu.VMEM((toks, span), BF16),
            ],
            compiler_params=params(),
            name=f"attend_half_{half}",
        )(*operands)

    half_cross = middle // 2
    cross = shapes(half_cross, rows, span)
    *first, layer = attend(0, cross + [pltpu.VMEM((toks, span), BF16)], len(cross), [])
    first = split(first, half_cross)
    got_first = [swap(first[k], middle + half_cross + k, n_seq) for k in range(half_cross)]
    far, near = shapes(half_cross, rows, width), shapes(middle, rows, width)
    outs = attend(1, cross + far + near, len(cross), [layer])
    second, outs = split(outs[: len(cross)], half_cross), outs[len(cross) :]
    far, near = split(outs[: len(far)], half_cross), split(outs[len(far) :], middle)
    got_far = [swap(far[k], middle + k, n_seq) for k in range(half_cross)]
    got_near = [near[0]] + [swap(near[k], k, n_seq) for k in range(1, middle)]
    got_second = [swap(second[k], middle + half_cross + k, n_seq) for k in range(half_cross)]

    def parts(found):
        if merged:
            pieces = [a[r : r + rows, c : c + span] for a, r, c in found]
            return [jnp.concatenate(pieces, axis=0)], [(0, 0, len(found) * rows, 0)]
        return [a for a, _, _ in found], [(i, r, rows, c) for i, (_, r, c) in enumerate(found)]

    near_parts = [[(a, 0, half * span) for a in got_near] for half in range(kvh)]
    cross_parts = [
        [(a, 0, half * span) for a in got_far] + [(a, 0, 0) for a in got]
        for half, got in enumerate((got_first, got_second))
    ]
    arrays, where = parts(near_parts[0])
    waits = got_first
    count = pl.pallas_call(
        functools.partial(count_kernel, 0, rows, where),
        out_shape=pltpu.VMEM((max(16, n_seq), 128), F32),
        in_specs=[vmem()] * len(arrays) + [pl.BlockSpec(memory_space=pl.ANY)] * len(waits),
        out_specs=vmem(),
        compiler_params=params(),
        name="count",
    )(*arrays, *waits)

    steps = 4
    cols = span // steps
    scratch = [pltpu.VMEM((steps, toks, cols), BF16), pltpu.SemaphoreType.DMA((steps,))]
    out_shape = jax.ShapeDtypeStruct((toks, width), BF16)
    anywhere = pl.BlockSpec(memory_space=pl.ANY)
    arrays, where = parts(near_parts[0] + cross_parts[0])
    out, sel = pl.pallas_call(
        functools.partial(place_kernel, n_seq, rows, middle, 0, where),
        out_shape=[out_shape, pltpu.VMEM((toks, n_seq * rows), BF16)],
        in_specs=[vmem()] * (1 + len(arrays)),
        out_specs=[anywhere, vmem()],
        scratch_shapes=scratch,
        compiler_params=params(),
        name="place_first",
    )(count, *arrays)
    arrays, where = parts(near_parts[1] + cross_parts[1])
    return pl.pallas_call(
        functools.partial(place_kernel, n_seq, rows, middle, 1, where),
        out_shape=out_shape,
        in_specs=[vmem()] * (1 + len(arrays)) + [anywhere],
        out_specs=anywhere,
        scratch_shapes=scratch,
        input_output_aliases={1 + len(arrays): 0},
        compiler_params=params(),
        name="place_second",
    )(sel, *arrays, out)


def solution(mesh):
    in_specs = (P(("dp", "seq"), None), P(), P(), P(), P(), P(), P(), P("dp"), P(("dp", "seq")))
    out_specs = P(("dp", "seq"), None)
    return jax.shard_map(
        per_device, mesh=mesh, in_specs=in_specs, out_specs=out_specs, check_vma=False
    )
```
